32 devices in a mesh: group: 2 (over y), gx: 4 (over z), gy: 4 (over x, core).
Axes of the slice: x: 2, y: 2, z: 4, core: 2. Of those that a mesh axis runs over, the one named last changes fastest.
Arguments:
- hidden_in: bfloat16 [128, 16384], P('group', ('gx', 'gy')), parts along dimension 0, may hold values from -6 to 6
- exponents: int32 [128, 128], P('group', 'gx'), parts along dimension 0, may hold values from -2 to 1
- signs: int32 [128], replicated, may hold values from 0 to 1
- lengths: int32 [128], P(('group', 'gx')), parts along dimension 0, may hold values from 1 to 1024, 32768 in all
- w_query: bfloat16 [16384, 8192], P('gx', 'gy'), may hold values from -0.046875 to 0.046875
- key_value_weight: bfloat16 [16384, 8, 2, 128], P('gx', 'gy'), may hold values from -0.046875 to 0.046875
- w_out: bfloat16 [8192, 16384], P('gy', 'gx'), may hold values from -0.0625 to 0.0625
- keys_cache: bfloat16 [128, 8, 1024, 128], P(('group', 'gx'), 'gy'), parts along dimension 0, may hold values from -600 to 600
- cached_value_rows: bfloat16 [128, 8, 1024, 128], P(('group', 'gx'), 'gy'), parts along dimension 0, may hold values from -24 to 24
Outputs:
- attn_update: bfloat16 [128, 16384], P('group', ('gx', 'gy')), parts along dimension 0
The draws below stay inside these ranges and needn't reach their ends.
There are 2 independent parts, one for each index of `group`. The reference program is written for one: setup_inputs(seed, part) draws one part's arguments, and reference() takes and returns one part's arrays. A program takes and returns all parts, laid end to end along the dimension named above; an argument that names none is the same for every part. Nothing has to cross between parts.
Inputs may be any that keep to these rules, and one draw needn't show every extreme that they name: `lengths`: the longest request of a part holds exactly 1024 cached tokens.
All inputs are finite; a program needn't handle non-finite values. No bound on the sum of `lengths` on one device may be relied on, other than what follows from the above.
Results may differ from the reference program's by a relative error of at most 0.0065.
The reference program's roundings to bfloat16 on the way count: a program that leaves them out, or rounds other values in their place, can miss the bound.
Values may be sent and summed in bfloat16 or wider, within the bound.
A program may use at most 128 MiB of HBM per device.

```python
import math
import jax
import jax.numpy as jnp
import numpy as np
from jax import lax

MODEL_WIDTH = 16384
QUERY_HEADS = 64
KEY_VALUE_HEADS = 8
HEAD_SIZE = 128
HB = 128
CACHE_SLOTS = 1024
REQUEST_TOTAL = 64


def draw_keys_cache(key, part):
    key = jax.random.fold_in(key, 11)
    sampled_draws = jnp.clip(jax.random.normal(key, (REQUEST_TOTAL, KEY_VALUE_HEADS, CACHE_SLOTS, HEAD_SIZE), jnp.float32) * 1.5, -9.0, 9.0)
    return sampled_draws.astype(jnp.bfloat16)


def with_ends(entries, own_key, low, top_value):
    spot = [jax.random.randint(jax.random.fold_in(own_key, axis), (), 0, length) for axis, length in enumerate(entries.shape)]
    widest = entries.shape.index(max(entries.shape))
    neighbour = spot[:widest] + [(spot[widest] + 1) % entries.shape[widest]] + spot[widest + 1:]
    return entries.at[tuple(spot)].set(low).at[tuple(neighbour)].set(top_value)


def block_scale(key, shape, pieces, low, top_value):
    level = 1.0
    for axis_at, blocks in pieces:
        heights = jax.random.uniform(jax.random.fold_in(jax.random.fold_in(key, 6), axis_at), (blocks,), jnp.float32, low / len(pieces), top_value / len(pieces))
        level = level * jnp.repeat(jnp.exp(heights), shape[axis_at] // blocks).reshape((-1,) + (1,) * (len(shape) - 1 - axis_at))
    return level


def profile(count, total, most, skew):
    portions = [(1 << 20) // math.isqrt(grade ** skew) + 1 for grade in range(2, count + 1)]
    surplus, given = total - most - (count - 1), [1] * (count - 1)
    while surplus > 0:
        free = [i for i in range(count - 1) if given[i] < most]
        mass, budget = sum([portions[i] for i in free]), surplus
        for i in free:
            extra = min(most - given[i], max(1, budget * portions[i] // mass), surplus)
            given[i] = given[i] + extra
            surplus = surplus - extra
    return np.array([most] + given)


def ragged(own_key, number_of, total, bound, slope):
    if number_of == 2:
        one = jax.random.randint(own_key, (), max(1, total - bound), min(bound, total - 1) + 1)
        return jnp.stack([one, total - one])
    tallies = jnp.asarray(profile(number_of, total, bound, slope), jnp.int32)
    pairs = (number_of - 1) // 2
    giver, receiver = tallies[1:1 + 2 * pairs:2], tallies[2:2 + 2 * pairs:2]
    slack = jnp.minimum(giver - 1, bound - receiver)
    passed = jax.random.randint(jax.random.fold_in(own_key, 1), (pairs,), 0, 1 << 20) % (slack + 1)
    tallies = tallies.at[1:1 + 2 * pairs:2].set(giver - passed).at[2:2 + 2 * pairs:2].set(receiver + passed)
    return tallies[jax.random.permutation(jax.random.fold_in(own_key, 2), number_of)]


def gaussian(own_key, extent, spread, most, split=(), held_as=jnp.bfloat16):
    drawn = spread * jax.random.normal(own_key, extent, jnp.float32)
    if split:
        drawn = drawn * block_scale(own_key, extent, split, -0.22, 0.18)
    return jnp.clip(drawn, -most, most).astype(held_as)


def setup_inputs(seed: int = 0, part: int = 0) -> dict:
    seeds = jax.random.split(jax.random.key(seed), 10)
    part_keys = jax.random.split(jax.random.fold_in(seeds[9], part), 10)
    hidden_in = gaussian(part_keys[0], (REQUEST_TOTAL, MODEL_WIDTH), 1.0, 6.0, ((1, 16),))
    exponents = with_ends(jax.random.randint(part_keys[1], (REQUEST_TOTAL, MODEL_WIDTH // HB), -2, 2), jax.random.fold_in(part_keys[1], 1), -2, 1).astype(jnp.int32)
    signs = with_ends(jax.random.randint(seeds[2], (HB,), 0, 2), jax.random.fold_in(seeds[2], 1), 0, 1).astype(jnp.int32)
    lengths = ragged(part_keys[3], REQUEST_TOTAL, REQUEST_TOTAL * CACHE_SLOTS // 2, CACHE_SLOTS, 0).astype(jnp.int32)
    w_query = gaussian(seeds[4], (MODEL_WIDTH, QUERY_HEADS * HEAD_SIZE), MODEL_WIDTH ** -0.5, 0.046875, ((0, 4), (1, 4)))
    key_value_weight = gaussian(seeds[5], (MODEL_WIDTH, KEY_VALUE_HEADS, 2, HEAD_SIZE), MODEL_WIDTH ** -0.5, 0.046875, ((0, 4), (1, 4)))
    w_out = gaussian(seeds[6], (QUERY_HEADS * HEAD_SIZE, MODEL_WIDTH), (QUERY_HEADS * HEAD_SIZE) ** -0.5, 0.0625, ((0, 4), (1, 4)))
    keys_cache = draw_keys_cache(jax.random.fold_in(jax.random.fold_in(seeds[9], part), 71), part)
    cached_value_rows = gaussian(part_keys[8], (REQUEST_TOTAL, KEY_VALUE_HEADS, CACHE_SLOTS, HEAD_SIZE), 4.0, 24.0, ((0, 4), (1, 4)))
    return dict(hidden_in=hidden_in, exponents=exponents, signs=signs, lengths=lengths, w_query=w_query, key_value_weight=key_value_weight, w_out=w_out, keys_cache=keys_cache, cached_value_rows=cached_value_rows)


def hadamard_table(block_len):
    index_vals = jnp.arange(block_len, dtype=jnp.int32)
    parity = jnp.zeros((block_len, block_len), jnp.int32)
    for bit_number in range(block_len.bit_length() - 1):
        step_size = 2 ** bit_number
        parity = parity + index_vals[:, None] // step_size % 2 * (index_vals[None, :] // step_size % 2)
    return jnp.where(parity % 2 == 0, 1.0, -1.0).astype(jnp.float32) / math.sqrt(block_len)

def quantize(blocks, exps, table, signs):
    signed = blocks * (2.0 * signs.astype(jnp.float32) - 1.0)
    rotated = jnp.einsum('bnk,kj->bnj', signed, table, precision=lax.Precision.HIGHEST)
    factor = jnp.exp2(exps.astype(jnp.float32))[..., None]
    coded = jnp.clip(rotated / factor, -4.0, 4.0).astype(jnp.bfloat16)
    return (coded.astype(jnp.float32) * factor).astype(jnp.bfloat16)

def rotary_angles(values, positions):
    half_width = values.shape[-1] // 2
    freqs = jnp.power(500000.0, -(jnp.arange(half_width, dtype=jnp.float32) * 2.0 / values.shape[-1]))
    angles = positions.astype(jnp.float32).reshape((-1,) + (1,) * (values.ndim - 1)) * freqs
    cosine = jnp.cos(angles)
    sine = jnp.sin(angles)
    first_half = values[..., :half_width]
    second_half = values[..., half_width:]
    return jnp.concatenate([first_half * cosine - second_half * sine, second_half * cosine + first_half * sine], axis=-1)

def attend_one(items):
    query_rotated, key_new, value_new, keys, values, length = items
    scale = 1.0 / math.sqrt(query_rotated.shape[-1])
    scores = jnp.einsum('grd,gpd->grp', query_rotated.astype(jnp.float32), keys.astype(jnp.float32)) * scale
    fresh = jnp.einsum('grd,gd->gr', query_rotated.astype(jnp.float32), key_new.astype(jnp.float32)) * scale
    valid = jnp.arange(keys.shape[1], dtype=jnp.int32) < length
    masked = jnp.where(valid, scores, -1e+30)
    top = jnp.maximum(lax.optimization_barrier(jnp.max(masked, axis=-1)), fresh)
    weights = jnp.where(valid, jnp.exp(masked - top[..., None]), 0.0)
    fresh_w = jnp.exp(fresh - top)
    total = lax.optimization_barrier(jnp.sum(weights, axis=-1)) + fresh_w
    probs = (weights / total[..., None]).astype(jnp.bfloat16)
    fresh_p = (fresh_w / total).astype(jnp.bfloat16)
    mixed = jnp.einsum('grp,gpd->grd', probs.astype(jnp.float32), values.astype(jnp.float32))
    mixed = mixed + fresh_p.astype(jnp.float32)[..., None] * value_new.astype(jnp.float32)[:, None, :]
    return mixed.astype(jnp.bfloat16)

def reference(hidden_in, exponents, signs, lengths, w_query, key_value_weight, w_out, keys_cache, cached_value_rows):
    widened = hidden_in.astype(jnp.float32)
    energy = lax.optimization_barrier(jnp.sum(widened * widened, axis=1, keepdims=True))
    normed = widened * lax.rsqrt(energy / MODEL_WIDTH + 1e-05)
    table = hadamard_table(HB)
    decoded_output = quantize(normed.reshape(REQUEST_TOTAL, MODEL_WIDTH // HB, HB), exponents, table, signs).reshape(REQUEST_TOTAL, MODEL_WIDTH)
    query_unrotated = jnp.dot(decoded_output, w_query, preferred_element_type=jnp.float32).reshape(REQUEST_TOTAL, QUERY_HEADS, HEAD_SIZE)
    key_value_unrotated = jnp.dot(decoded_output, key_value_weight.reshape(MODEL_WIDTH, KEY_VALUE_HEADS * 2 * HEAD_SIZE), preferred_element_type=jnp.float32).reshape(REQUEST_TOTAL, KEY_VALUE_HEADS, 2, HEAD_SIZE)
    query_rotated = rotary_angles(query_unrotated, lengths).astype(jnp.bfloat16).reshape(REQUEST_TOTAL, KEY_VALUE_HEADS, QUERY_HEADS // KEY_VALUE_HEADS, HEAD_SIZE)
    key_new = rotary_angles(key_value_unrotated[:, :, 0], lengths).astype(jnp.bfloat16)
    value_new = key_value_unrotated[:, :, 1].astype(jnp.bfloat16)
    attended = lax.map(attend_one, (query_rotated, key_new, value_new, keys_cache, cached_value_rows, lengths))
    return jnp.dot(attended.reshape(REQUEST_TOTAL, QUERY_HEADS * HEAD_SIZE), w_out, preferred_element_type=jnp.float32).astype(jnp.bfloat16)
```

```python
import functools
import math

import jax
import jax.numpy as jnp
from jax import lax
from jax.experimental import pallas as pl
from jax.experimental.pallas import tpu as pltpu
from jax.sharding import PartitionSpec as P

MODEL_WIDTH = 16384
MESH = pl.DeviceIdType.MESH
CHUNK = 512


def decode_kernel(
    nx, ny, dims,
    hidden_ref, exps_ref, signs_ref, cos_ref, sin_ref, len_ref,
    wq_hbm, kv_hbm, wout_hbm, keys_hbm, values_hbm,
    out_ref,
    wbuf, kv_raw, kv_stage, kv_w, keys, values,
    hid, en, dec, part, got, q2d, kv2d, att2d, att_all, term, terms_in,
    w_sem, kv_sem, k_sem, v_sem, wo_sem,
    hs_sem, hr_sem, es_sem, er_sem, ps_sem, pr_sem, as_sem, ar_sem, ts_sem, tr_sem,
):
    batch, feat, q_cols, owners, kv_heads, reps, slots, head_dim, out_cols = dims
    gx = lax.axis_index("gx")
    gy = lax.axis_index("gy")
    peers = nx * ny
    me = gx * ny + gy
    block = head_dim
    q_chunks = q_cols // CHUNK
    depth = feat * ny
    heads = kv_heads * reps
    f32, bf16 = jnp.float32, jnp.bfloat16

    def kv_copy():
        return pltpu.make_async_copy(kv_hbm, kv_raw, kv_sem)

    def wq_copy(c):
        return pltpu.make_async_copy(
            wq_hbm.at[:, pl.ds(pl.multiple_of(c * CHUNK, CHUNK), CHUNK)], wbuf.at[c], w_sem.at[c]
        )

    kv_copy().start()
    for c in range(q_chunks):
        wq_copy(c).start()
    k_copy = pltpu.make_async_copy(keys_hbm, keys, k_sem)
    v_copy = pltpu.make_async_copy(values_hbm, values, v_sem)
    k_copy.start()
    v_copy.start()

    barrier = pltpu.get_barrier_semaphore()

    def peer(k):
        idx = lax.rem(me + k, peers)
        return {"gx": idx // ny, "gy": lax.rem(idx, ny)}

    def greet(k, carry):
        pl.semaphore_signal(barrier, inc=1, device_id=peer(k), device_id_type=MESH)
        return carry

    lax.fori_loop(1, peers, greet, 0)

    own = hidden_ref[...]
    wide = own.astype(f32)
    square = wide * wide
    high = square.astype(bf16)
    low = (square - high.astype(f32)).astype(bf16)
    ones = jnp.ones((8, feat), bf16)
    contract = (((1,), (1,)), ((), ()))
    row = lax.dot_general(ones, high, contract, preferred_element_type=f32) + lax.dot_general(
        ones, low, contract, preferred_element_type=f32
    )
    lanes = en.shape[2]
    if lanes > batch:
        row = jnp.concatenate([row, jnp.zeros((8, lanes - batch), f32)], axis=1)
    en[me] = row
    hid[gy] = own

    pl.semaphore_wait(barrier, peers - 1)

    def energy_copy(k):
        return pltpu.make_async_remote_copy(
            src_ref=en.at[me], dst_ref=en.at[me], send_sem=es_sem.at[k - 1],
            recv_sem=er_sem.at[k - 1], device_id=peer(k), device_id_type=MESH,
        )

    def send_energy(k, carry):
        energy_copy(k).start()
        return carry

    lax.fori_loop(1, peers, send_energy, 0)

    def hidden_copy(d):
        return pltpu.make_async_remote_copy(
            src_ref=hid.at[gy], dst_ref=hid.at[gy], send_sem=hs_sem.at[d - 1],
            recv_sem=hr_sem.at[d - 1], device_id={"gy": lax.rem(gy + d, ny)}, device_id_type=MESH,
        )

    for d in range(1, ny):
        hidden_copy(d).start()

    kv_copy().wait()
    parts = kv_heads * 2
    step_rows = kv_stage.shape[0]
    rows_out = step_rows // parts

    def separate(i, carry):
        base = pl.multiple_of(i * step_rows, step_rows)
        kv_stage[...] = kv_raw[pl.ds(base, step_rows), :].astype(f32)
        to = pl.multiple_of(i * rows_out, rows_out)
        for j in range(parts):
            kv_w[pl.ds(to, rows_out), j * head_dim:(j + 1) * head_dim] = kv_stage[
                pl.ds(j, rows_out, stride=parts), :
            ].astype(bf16)
        return carry

    lax.fori_loop(0, depth // rows_out, separate, 0)

    r = lax.broadcasted_iota(jnp.int32, (block, block), 0)
    c = lax.broadcasted_iota(jnp.int32, (block, block), 1)
    common = r & c
    parity = jnp.zeros((block, block), jnp.int32)
    for bit in range(block.bit_length() - 1):
        parity = parity + ((common >> bit) & 1)
    sign_row = 2.0 * signs_ref[...].astype(f32) - 1.0
    sign_col = jnp.sum(jnp.where(r == c, sign_row, 0.0), axis=1, keepdims=True)
    table = (jnp.where((parity & 1) == 0, 1.0, -1.0) * sign_col).astype(bf16)

    def wait_energy(k, carry):
        energy_copy(k).wait()
        return carry

    lax.fori_loop(1, peers, wait_energy, 0)
    energy_row = jnp.sum(en[...], axis=0)[0:1, :]
    er = lax.broadcasted_iota(jnp.int32, (batch, lanes), 0)
    ec = lax.broadcasted_iota(jnp.int32, (batch, lanes), 1)
    energy = jnp.sum(jnp.where(er == ec, energy_row, 0.0), axis=1, keepdims=True)
    scale_col = lax.rsqrt(energy / MODEL_WIDTH + 1e-05) * (1.0 / math.sqrt(block))
    exps = exps_ref[...]
    factors = jnp.where(
        exps >= 0, jnp.where(exps >= 1, 2.0, 1.0), jnp.where(exps >= -1, 0.5, 0.25)
    ).astype(f32)
    inverses = 1.0 / factors
    blocks_each = feat // block
    which = lax.broadcasted_iota(jnp.int32, exps.shape, 1)

    def code(src):
        for b in range(blocks_each):
            n = src * blocks_each + b
            pick = which == n
            factor = jnp.sum(jnp.where(pick, factors, 0.0), axis=1, keepdims=True)
            inverse = jnp.sum(jnp.where(pick, inverses, 0.0), axis=1, keepdims=True)
            raw = jnp.dot(
                hid[src, :, b * block:(b + 1) * block], table, preferred_element_type=f32
            )
            coded = jnp.clip(raw * scale_col * inverse, -4.0, 4.0).astype(bf16)
            dec[src, :, b * block:(b + 1) * block] = (coded.astype(f32) * factor).astype(bf16)

    code(gy)
    for d in range(1, ny):
        hidden_copy(d).wait()
        code(lax.rem(gy + ny - d, ny))

    def part_copy(ch, d):
        to = lax.rem(gx + d, nx)
        return pltpu.make_async_remote_copy(
            src_ref=part.at[ch, to], dst_ref=got.at[ch, gx], send_sem=ps_sem.at[ch, d - 1],
            recv_sem=pr_sem.at[ch, d - 1], device_id={"gx": to}, device_id_type=MESH,
        )

    def ship(ch, total):
        for j in range(nx):
            part[ch, j] = total[j * owners:(j + 1) * owners]
        for d in range(1, nx):
            part_copy(ch, d).start()

    def project(read):
        total = jnp.zeros((batch, CHUNK), f32)
        for s in range(ny):
            total = total + jnp.dot(dec[s], read(s), preferred_element_type=f32)
        return total

    ship(q_chunks, project(lambda s: kv_w[s * feat:(s + 1) * feat, :]))

    def q_step(ch, carry):
        wq_copy(ch).wait()
        ship(ch, project(lambda s: wbuf[ch, s * feat:(s + 1) * feat, :]))
        return carry

    lax.fori_loop(0, q_chunks, q_step, 0)

    wo_rows = wout_hbm.shape[0]
    halves = depth // wo_rows
    wo_wide = halves * CHUNK

    def wo_copy(j, h):
        return pltpu.make_async_copy(
            wout_hbm.at[:, pl.ds(pl.multiple_of(j * wo_wide + h * CHUNK, CHUNK), CHUNK)],
            wbuf.at[j, pl.ds(h * wo_rows, wo_rows)],
            wo_sem.at[j, h],
        )

    for j in range(ny):
        for h in range(halves):
            wo_copy(j, h).start()

    cosine = cos_ref[...]
    sine = sin_ref[...]

    def rope(v):
        return v * cosine + pltpu.roll(v, head_dim // 2, 1) * sine

    def arrived(ch):
        for d in range(1, nx):
            part_copy(ch, d).wait_recv()
        total = part[ch, gx]
        for d in range(1, nx):
            total = total + got[ch, lax.rem(gx + d, nx)]
        return total

    per = CHUNK // head_dim
    total = arrived(q_chunks)
    for j in range(parts):
        v = total[:, j * head_dim:(j + 1) * head_dim]
        if j % 2 == 0:
            v = rope(v)
        kv2d[j * owners:(j + 1) * owners, :] = v.astype(bf16).astype(f32)

    for ch in range(q_chunks):
        total = arrived(ch)
        for j in range(per):
            h = ch * per + j
            v = rope(total[:, j * head_dim:(j + 1) * head_dim])
            q2d[h * owners:(h + 1) * owners, :] = v.astype(bf16).astype(f32)

    k_copy.wait()
    v_copy.wait()
    factor = 1.0 / math.sqrt(head_dim)
    position = lax.broadcasted_iota(jnp.int32, (reps, slots), 1)
    group = 4

    def attend(i, carry):
        scores, fresh, mask, new_v = [], [], [], []
        for jb in range(group):
            b = i * group + jb
            length = len_ref[b]
            for g in range(kv_heads):
                q = q2d[pl.ds(g * reps * owners + b, reps, stride=owners), :]
                k_new = kv2d[pl.ds(2 * g * owners + b, 1), :]
                new_v.append(kv2d[pl.ds((2 * g + 1) * owners + b, 1), :])
                scores.append(
                    lax.dot_general(
                        q.astype(bf16), keys[b * kv_heads + g], contract,
                        preferred_element_type=f32,
                    )
                )
                fresh.append(jnp.sum(q * k_new, axis=1, keepdims=True))
                mask.append(position < length)
        for n in range(group * kv_heads):
            b = i * group + n // kv_heads
            g = n % kv_heads
            f = fresh[n] * factor
            s = jnp.where(mask[n], scores[n] * factor, -1e30)
            top = jnp.maximum(jnp.max(s, axis=1, keepdims=True), f)
            w = jnp.where(mask[n], jnp.exp(s - top), 0.0)
            fw = jnp.exp(f - top)
            whole = jnp.sum(w, axis=1, keepdims=True) + fw
            probs = (w / whole).astype(bf16)
            fp = (fw / whole).astype(bf16).astype(f32)
            mixed = jnp.dot(probs, values[b * kv_heads + g], preferred_element_type=f32)
            mixed = mixed + fp * new_v[n]
            att2d[pl.ds(g * reps * owners + b, reps, stride=owners), :] = mixed
        return carry

    lax.fori_loop(0, owners // group, attend, 0)
    for h in range(heads):
        att_all[gx, :, h * head_dim:(h + 1) * head_dim] = att2d[
            h * owners:(h + 1) * owners, :
        ].astype(bf16)

    def att_copy(d):
        return pltpu.make_async_remote_copy(
            src_ref=att_all.at[gx], dst_ref=att_all.at[gx], send_sem=as_sem.at[d - 1],
            recv_sem=ar_sem.at[d - 1], device_id={"gx": lax.rem(gx + d, nx)}, device_id_type=MESH,
        )

    for d in range(1, nx):
        att_copy(d).start()
    for ch in range(q_chunks + 1):
        for d in range(1, nx):
            part_copy(ch, d).wait_send()
    for j in range(ny):
        for h in range(halves):
            wo_copy(j, h).wait()
    for d in range(1, nx):
        att_copy(d).wait()
    attended = att_all[...].reshape(batch, heads * head_dim)

    def term_copy(d, h):
        to = lax.rem(gy + d, ny)
        return pltpu.make_async_remote_copy(
            src_ref=term.at[to, h], dst_ref=terms_in.at[gy, h], send_sem=ts_sem.at[d - 1, h],
            recv_sem=tr_sem.at[d - 1, h], device_id={"gy": to}, device_id_type=MESH,
        )

    def out_piece(to, h):
        term[to, h] = jnp.dot(
            attended, wbuf[to, h * wo_rows:(h + 1) * wo_rows, :], preferred_element_type=f32
        )

    def out_step(d, carry):
        for h in range(halves):
            out_piece(lax.rem(gy + d, ny), h)
            term_copy(d, h).start()
        return carry

    lax.fori_loop(1, ny, out_step, 0)
    for h in range(halves):
        out_piece(gy, h)
    for h in range(halves):
        total = term[gy, h]
        for d in range(1, ny):
            term_copy(d, h).wait()
            total = total + terms_in[lax.rem(gy + ny - d, ny), h]
        out_ref[:, h * CHUNK:(h + 1) * CHUNK] = total.astype(bf16)


def direct_body(
    nx, ny, hidden_in, exponents, signs, lengths, w_query, key_value_weight, w_out,
    keys_cache, cached_value_rows,
):
    batch, feat = hidden_in.shape
    depth, q_cols = w_query.shape
    kv_heads, head_dim = key_value_weight.shape[1], key_value_weight.shape[3]
    owners = batch // nx
    heads = q_cols // head_dim
    reps = heads // kv_heads
    slots = keys_cache.shape[2]
    out_cols = w_out.shape[1]
    parts = 2 * kv_heads
    half = head_dim // 2
    freqs = jnp.power(500000.0, -(jnp.arange(half, dtype=jnp.float32) * 2.0 / head_dim))
    angles = lengths.astype(jnp.float32)[:, None] * freqs
    cosine, sine = jnp.cos(angles), jnp.sin(angles)
    cos_full = jnp.concatenate([cosine, cosine], axis=1)
    sin_full = jnp.concatenate([-sine, sine], axis=1)
    q_chunks = q_cols // CHUNK
    halves = depth // w_out.shape[0]
    dims = (batch, feat, q_cols, owners, kv_heads, reps, slots, head_dim, out_cols)
    vmem = pl.BlockSpec(memory_space=pltpu.VMEM)
    anyw = pl.BlockSpec(memory_space=pl.ANY)
    f32, bf16 = jnp.float32, jnp.bfloat16
    dma = pltpu.SemaphoreType.DMA
    lanes = max(batch, 128)
    return pl.pallas_call(
        functools.partial(decode_kernel, nx, ny, dims),
        out_shape=jax.ShapeDtypeStruct((batch, feat), bf16),
        in_specs=[vmem] * 5 + [pl.BlockSpec(memory_space=pltpu.SMEM)] + [anyw] * 5,
        out_specs=vmem,
        scratch_shapes=[
            pltpu.VMEM((q_chunks, depth, CHUNK), bf16),
            pltpu.VMEM((depth * parts, head_dim), bf16),
            pltpu.VMEM((1024, head_dim), f32),
            pltpu.VMEM((depth, parts * head_dim), bf16),
            pltpu.VMEM((owners * kv_heads, slots, head_dim), bf16),
            pltpu.VMEM((owners * kv_heads, slots, head_dim), bf16),
            pltpu.VMEM((ny, batch, feat), bf16),
            pltpu.VMEM((nx * ny, 8, lanes), f32),
            pltpu.VMEM((ny, batch, feat), bf16),
            pltpu.VMEM((q_chunks + 1, nx, owners, CHUNK), f32),
            pltpu.VMEM((q_chunks + 1, nx, owners, CHUNK), f32),
            pltpu.VMEM((heads * owners, head_dim), f32),
            pltpu.VMEM((parts * owners, head_dim), f32),
            pltpu.VMEM((heads * owners, head_dim), f32),
            pltpu.VMEM((nx, owners, heads * head_dim), bf16),
            pltpu.VMEM((ny, halves, batch, CHUNK), f32),
            pltpu.VMEM((ny, halves, batch, CHUNK), f32),
            dma((q_chunks,)), dma, dma, dma, dma((ny, halves)),
            dma((ny - 1,)), dma((ny - 1,)),
            dma((nx * ny - 1,)), dma((nx * ny - 1,)),
            dma((q_chunks + 1, nx - 1)), dma((q_chunks + 1, nx - 1)),
            dma((nx - 1,)), dma((nx - 1,)),
            dma((ny - 1, halves)), dma((ny - 1, halves)),
        ],
        compiler_params=pltpu.CompilerParams(
            collective_id=0, has_side_effects=True, vmem_limit_bytes=56 * 1024 * 1024
        ),
    )(
        hidden_in, exponents, signs.reshape(1, -1), cos_full, sin_full, lengths,
        w_query, key_value_weight.reshape(-1, head_dim), w_out,
        keys_cache.reshape(-1, slots, head_dim), cached_value_rows.reshape(-1, slots, head_dim),
    )


def hadamard_table(block_len):
    index_vals = jnp.arange(block_len, dtype=jnp.int32)
    parity = jnp.zeros((block_len, block_len), jnp.int32)
    for bit_number in range(block_len.bit_length() - 1):
        step_size = 2**bit_number
        parity = parity + index_vals[:, None] // step_size % 2 * (
            index_vals[None, :] // step_size % 2
        )
    return jnp.where(parity % 2 == 0, 1.0, -1.0).astype(jnp.float32) / math.sqrt(block_len)


def quantize(blocks, exps, table, signs):
    signed = blocks * (2.0 * signs.astype(jnp.float32) - 1.0)
    rotated = jnp.einsum("bnk,kj->bnj", signed, table, precision=lax.Precision.HIGHEST)
    factor = jnp.exp2(exps.astype(jnp.float32))[..., None]
    coded = jnp.clip(rotated / factor, -4.0, 4.0).astype(jnp.bfloat16)
    return (coded.astype(jnp.float32) * factor).astype(jnp.bfloat16)


def rotary_angles(values, positions):
    half_width = values.shape[-1] // 2
    freqs = jnp.power(
        500000.0, -(jnp.arange(half_width, dtype=jnp.float32) * 2.0 / values.shape[-1])
    )
    angles = positions.astype(jnp.float32).reshape((-1,) + (1,) * (values.ndim - 1)) * freqs
    cosine = jnp.cos(angles)
    sine = jnp.sin(angles)
    first_half = values[..., :half_width]
    second_half = values[..., half_width:]
    return jnp.concatenate(
        [first_half * cosine - second_half * sine, second_half * cosine + first_half * sine],
        axis=-1,
    )


def body(
    hidden_in,
    exponents,
    signs,
    lengths,
    w_query,
    key_value_weight,
    w_out,
    keys_cache,
    cached_value_rows,
):
    batch_all, local_feat = hidden_in.shape
    block_len = signs.shape[0]
    table = hadamard_table(block_len)
    widened = hidden_in.astype(jnp.float32)
    energy = lax.psum(jnp.sum(widened * widened, axis=1, keepdims=True), ("gx", "gy"))
    row_scale = lax.rsqrt(energy / MODEL_WIDTH + 1e-05)
    own_blocks = local_feat // block_len
    own_exps = lax.dynamic_slice_in_dim(exponents, lax.axis_index("gy") * own_blocks, own_blocks, 1)
    coded_own = quantize(
        (widened * row_scale).reshape(batch_all, own_blocks, block_len), own_exps, table, signs
    )
    gathered = lax.all_gather(coded_own.reshape(batch_all, local_feat), "gy", axis=1, tiled=True)
    query_cols = w_query.shape[1]
    kv_heads = key_value_weight.shape[1]
    head_dim = key_value_weight.shape[3]
    kv_flat = key_value_weight.reshape(key_value_weight.shape[0], kv_heads * 2 * head_dim)
    owners = batch_all // lax.axis_size("gx")
    partial_cols = lax.psum_scatter(
        jnp.concatenate(
            [
                jnp.dot(gathered, w_query, preferred_element_type=jnp.float32),
                jnp.dot(gathered, kv_flat, preferred_element_type=jnp.float32),
            ],
            axis=1,
        ),
        "gx",
        scatter_dimension=1,
        tiled=True,
    )
    mine = lax.all_to_all(partial_cols, "gx", split_axis=0, concat_axis=1, tiled=True)
    query_unrotated = mine[:, :query_cols].reshape(owners, kv_heads, -1, head_dim)
    key_value_unrotated = mine[:, query_cols:].reshape(owners, kv_heads, 2, head_dim)
    query_rotated = rotary_angles(query_unrotated, lengths).astype(jnp.bfloat16)
    key_new = rotary_angles(key_value_unrotated[:, :, 0], lengths).astype(jnp.bfloat16)
    value_new = key_value_unrotated[:, :, 1].astype(jnp.bfloat16)
    scale = 1.0 / math.sqrt(head_dim)
    scores = (
        jnp.einsum("bgrd,bgpd->bgrp", query_rotated, keys_cache, preferred_element_type=jnp.float32)
        * scale
    )
    fresh = (
        jnp.einsum("bgrd,bgd->bgr", query_rotated, key_new, preferred_element_type=jnp.float32)
        * scale
    )
    valid = (jnp.arange(keys_cache.shape[2], dtype=jnp.int32)[None, :] < lengths[:, None])[
        :, None, None, :
    ]
    masked = jnp.where(valid, scores, -1e30)
    top = jnp.maximum(jnp.max(masked, axis=-1), fresh)
    weights = jnp.where(valid, jnp.exp(masked - top[..., None]), 0.0)
    fresh_w = jnp.exp(fresh - top)
    total = jnp.sum(weights, axis=-1) + fresh_w
    probs = (weights / total[..., None]).astype(jnp.bfloat16)
    fresh_p = (fresh_w / total).astype(jnp.bfloat16)
    mixed = jnp.einsum(
        "bgrp,bgpd->bgrd", probs, cached_value_rows, preferred_element_type=jnp.float32
    )
    mixed = (
        mixed
        + fresh_p.astype(jnp.float32)[..., None] * value_new.astype(jnp.float32)[:, :, None, :]
    )
    attended = mixed.astype(jnp.bfloat16).reshape(owners, -1)
    terms = jnp.dot(
        lax.all_gather(attended, "gx", axis=0, tiled=True),
        w_out,
        preferred_element_type=jnp.float32,
    )
    summed = lax.psum_scatter(terms, "gy", scatter_dimension=1, tiled=True)
    return summed.astype(jnp.bfloat16)


def solution(mesh):
    in_specs = (
        P("group", ("gx", "gy")),
        P("group", "gx"),
        P(),
        P(("group", "gx")),
        P("gx", "gy"),
        P("gx", "gy", None, None),
        P("gy", "gx"),
        P(("group", "gx"), "gy", None, None),
        P(("group", "gx"), "gy", None, None),
    )
    out_specs = P("group", ("gx", "gy"))
    nx, ny = mesh.shape["gx"], mesh.shape["gy"]
    run = functools.partial(direct_body, nx, ny) if nx * ny <= 16 else body
    return jax.shard_map(run, mesh=mesh, in_specs=in_specs, out_specs=out_specs, check_vma=False)
```

```python
import functools
import math

import jax
import jax.numpy as jnp
import numpy as np
from jax import lax
from jax.experimental import pallas as pl
from jax.experimental.pallas import tpu as pltpu
from jax.sharding import PartitionSpec as P

MODEL_WIDTH = 16384
MESH = pl.DeviceIdType.MESH
CHUNK = 512


def decode_kernel(
    nx, ny, dims,
    hidden_ref, exps_ref, signs_ref, freq_ref, len_row_ref, len_ref,
    wq_hbm, kv_hbm, wout_hbm, keys_hbm, values_hbm,
    out_ref,
    wbuf, kv_raw, kv_stage, kv_w, keys, values,
    hid, en, dec, part, got, q2d, kv2d, att2d, att_all, term, pair_in, cross_in,
    w_sem, kv_sem, k_sem, v_sem, wo_sem,
    hs_sem, hr_sem, es_sem, er_sem, ps_sem, pr_sem, as_sem, ar_sem,
    ts_sem, tr_sem, xs_sem, xr_sem,
):
    batch, feat, q_cols, owners, kv_heads, reps, slots, head_dim, out_cols = dims
    gx = lax.axis_index("gx")
    gy = lax.axis_index("gy")
    peers = nx * ny
    chips = ny // 2
    chip, core = gy // 2, lax.rem(gy, 2)
    buddy = chip * 2 + 1 - core
    me = gx * ny + gy
    block = head_dim
    q_chunks = q_cols // CHUNK
    depth = feat * ny
    heads = kv_heads * reps
    f32, bf16 = jnp.float32, jnp.bfloat16

    def kv_copy():
        return pltpu.make_async_copy(kv_hbm, kv_raw, kv_sem)

    def wq_copy(c):
        return pltpu.make_async_copy(
            wq_hbm.at[:, pl.ds(pl.multiple_of(c * CHUNK, CHUNK), CHUNK)], wbuf.at[c], w_sem.at[c]
        )

    kv_copy().start()
    for c in range(q_chunks):
        wq_copy(c).start()
    k_copy = pltpu.make_async_copy(keys_hbm, keys, k_sem)
    v_copy = pltpu.make_async_copy(values_hbm, values, v_sem)
    k_copy.start()
    v_copy.start()

    barrier = pltpu.get_barrier_semaphore()

    def peer(k):
        idx = lax.rem(me + k, peers)
        return {"gx": idx // ny, "gy": lax.rem(idx, ny)}

    def greet(k, carry):
        pl.semaphore_signal(barrier, inc=1, device_id=peer(k), device_id_type=MESH)
        return carry

    lax.fori_loop(1, peers, greet, 0)

    own = hidden_ref[...]
    wide = own.astype(f32)
    square = wide * wide
    high = square.astype(bf16)
    low = (square - high.astype(f32)).astype(bf16)
    ones = jnp.ones((8, feat), bf16)
    contract = (((1,), (1,)), ((), ()))
    row = lax.dot_general(ones, high, contract, preferred_element_type=f32) + lax.dot_general(
        ones, low, contract, preferred_element_type=f32
    )
    lanes = en.shape[2]
    if lanes > batch:
        row = jnp.concatenate([row, jnp.zeros((8, lanes - batch), f32)], axis=1)
    en[me] = row
    hid[gy] = own

    pl.semaphore_wait(barrier, peers - 1)

    def energy_copy(k):
        return pltpu.make_async_remote_copy(
            src_ref=en.at[me], dst_ref=en.at[me], send_sem=es_sem.at[k - 1],
            recv_sem=er_sem.at[k - 1], device_id=peer(k), device_id_type=MESH,
        )

    def send_energy(k, carry):
        energy_copy(k).start()
        return carry

    def across(e):
        return lax.rem(chip + e, chips) * 2 + core

    def hidden_copy(n):
        src = gy if n < chips else lax.rem(chip + chips - (n - chips + 1), chips) * 2 + core
        to = across(n) if 1 <= n < chips else buddy
        return pltpu.make_async_remote_copy(
            src_ref=hid.at[src], dst_ref=hid.at[src], send_sem=hs_sem.at[n],
            recv_sem=hr_sem.at[n], device_id={"gy": to}, device_id_type=MESH,
        )

    for e in range(1, chips):
        hidden_copy(e).start()
    lax.fori_loop(1, peers, send_energy, 0)
    hidden_copy(0).start()

    lr = lax.broadcasted_iota(jnp.int32, (owners, owners), 0)
    lc = lax.broadcasted_iota(jnp.int32, (owners, owners), 1)
    place = jnp.sum(
        jnp.where(lr == lc, len_row_ref[...].astype(f32), 0.0), axis=1, keepdims=True
    )
    angles = place * freq_ref[...]
    first = lax.broadcasted_iota(jnp.int32, (owners, head_dim), 1) < head_dim // 2
    cosine = jnp.cos(angles)
    sine = jnp.where(first, -1.0, 1.0) * jnp.sin(angles)

    kv_copy().wait()
    parts = kv_heads * 2
    step_rows = kv_stage.shape[0]
    rows_out = step_rows // parts

    def separate(i, carry):
        base = pl.multiple_of(i * step_rows, step_rows)
        kv_stage[...] = kv_raw[pl.ds(base, step_rows), :].astype(f32)
        to = pl.multiple_of(i * rows_out, rows_out)
        for j in range(parts):
            kv_w[pl.ds(to, rows_out), j * head_dim:(j + 1) * head_dim] = kv_stage[
                pl.ds(j, rows_out, stride=parts), :
            ].astype(bf16)
        return carry

    lax.fori_loop(0, depth // rows_out, separate, 0)

    r = lax.broadcasted_iota(jnp.int32, (block, block), 0)
    c = lax.broadcasted_iota(jnp.int32, (block, block), 1)
    common = r & c
    parity = jnp.zeros((block, block), jnp.int32)
    for bit in range(block.bit_length() - 1):
        parity = parity + ((common >> bit) & 1)
    sign_row = 2.0 * signs_ref[...].astype(f32) - 1.0
    sign_col = jnp.sum(jnp.where(r == c, sign_row, 0.0), axis=1, keepdims=True)
    table = (jnp.where((parity & 1) == 0, 1.0, -1.0) * sign_col).astype(bf16)

    for e in range(1, chips):
        hidden_copy(e).wait_recv()
        hidden_copy(chips - 1 + e).start()

    def wait_energy(k, carry):
        energy_copy(k).wait()
        return carry

    lax.fori_loop(1, peers, wait_energy, 0)
    energy_row = jnp.sum(en[...], axis=0)[0:1, :]
    er = lax.broadcasted_iota(jnp.int32, (batch, lanes), 0)
    ec = lax.broadcasted_iota(jnp.int32, (batch, lanes), 1)
    energy = jnp.sum(jnp.where(er == ec, energy_row, 0.0), axis=1, keepdims=True)
    scale_col = lax.rsqrt(energy / MODEL_WIDTH + 1e-05) * (1.0 / math.sqrt(block))
    blocks_each = feat // block
    own_lane = lax.broadcasted_iota(jnp.int32, (batch, batch), 0) == lax.broadcasted_iota(
        jnp.int32, (batch, batch), 1
    )

    def code(src):
        for b in range(blocks_each):
            n = src * blocks_each + b
            exps = exps_ref[pl.ds(n, 1), :]
            factors = jnp.where(
                exps >= 0, jnp.where(exps >= 1, 2.0, 1.0), jnp.where(exps >= -1, 0.5, 0.25)
            )
            factor = jnp.sum(jnp.where(own_lane, factors, 0.0), axis=1, keepdims=True)
            inverse = 1.0 / factor
            raw = jnp.dot(
                hid[src, :, b * block:(b + 1) * block], table, preferred_element_type=f32
            )
            coded = jnp.clip(raw * scale_col * inverse, -4.0, 4.0).astype(bf16)
            dec[src, :, b * block:(b + 1) * block] = (coded.astype(f32) * factor).astype(bf16)

    code(gy)
    for e in range(1, chips):
        code(lax.rem(chip + chips - e, chips) * 2 + core)
    hidden_copy(0).wait_recv()
    code(buddy)
    for e in range(1, chips):
        hidden_copy(chips - 1 + e).wait_recv()
        code(lax.rem(chip + chips - e, chips) * 2 + 1 - core)
    for n in range(ny - 1):
        hidden_copy(n).wait_send()

    def part_copy(ch, d):
        to = lax.rem(gx + d, nx)
        return pltpu.make_async_remote_copy(
            src_ref=part.at[ch, to], dst_ref=got.at[ch, gx], send_sem=ps_sem.at[ch, d - 1],
            recv_sem=pr_sem.at[ch, d - 1], device_id={"gx": to}, device_id_type=MESH,
        )

    def ship(ch, total):
        for j in range(nx):
            part[ch, j] = total[j * owners:(j + 1) * owners]
        for d in range(1, nx):
            part_copy(ch, d).start()

    def project(read):
        total = jnp.zeros((batch, CHUNK), f32)
        for s in range(ny):
            total = total + jnp.dot(dec[s], read(s), preferred_element_type=f32)
        return total

    ship(q_chunks, project(lambda s: kv_w[s * feat:(s + 1) * feat, :]))

    def q_step(ch, carry):
        wq_copy(ch).wait()
        ship(ch, project(lambda s: wbuf[ch, s * feat:(s + 1) * feat, :]))
        return carry

    lax.fori_loop(0, q_chunks, q_step, 0)

    wo_rows = wout_hbm.shape[0]
    halves = depth // wo_rows
    wo_wide = halves * CHUNK

    def wo_copy(j, h):
        return pltpu.make_async_copy(
            wout_hbm.at[:, pl.ds(pl.multiple_of(j * wo_wide + h * CHUNK, CHUNK), CHUNK)],
            wbuf.at[j, pl.ds(h * wo_rows, wo_rows)],
            wo_sem.at[j, h],
        )

    for j in range(ny):
        for h in range(halves):
            wo_copy(j, h).start()

    def rope(v):
        return v * cosine + pltpu.roll(v, head_dim // 2, 1) * sine

    def arrived(ch):
        for d in range(1, nx):
            part_copy(ch, d).wait_recv()
        total = part[ch, gx]
        for d in range(1, nx):
            total = total + got[ch, lax.rem(gx + d, nx)]
        return total

    per = CHUNK // head_dim
    total = arrived(q_chunks)
    for j in range(parts):
        v = total[:, j * head_dim:(j + 1) * head_dim]
        if j % 2 == 0:
            v = rope(v)
        kv2d[j * owners:(j + 1) * owners, :] = v.astype(bf16).astype(f32)

    for ch in range(q_chunks):
        total = arrived(ch)
        for j in range(per):
            h = ch * per + j
            v = rope(total[:, j * head_dim:(j + 1) * head_dim])
            q2d[h * owners:(h + 1) * owners, :] = v.astype(bf16).astype(f32)

    k_copy.wait()
    v_copy.wait()
    factor = 1.0 / math.sqrt(head_dim)
    position = lax.broadcasted_iota(jnp.int32, (reps, slots), 1)
    group = 8

    def attend(g, i, carry):
        scores, fresh, mask, new_v = [], [], [], []
        for jb in range(group):
            b = i * group + jb
            q = q2d[pl.ds(g * reps * owners + b, reps, stride=owners), :]
            k_new = kv2d[pl.ds(2 * g * owners + b, 1), :]
            new_v.append(kv2d[pl.ds((2 * g + 1) * owners + b, 1), :])
            scores.append(
                lax.dot_general(
                    q.astype(bf16), keys[b * kv_heads + g], contract, preferred_element_type=f32
                )
            )
            fresh.append(jnp.sum(q * k_new, axis=1, keepdims=True))
            mask.append(position < len_ref[b])
        for n in range(group):
            b = i * group + n
            f = fresh[n] * factor
            s = jnp.where(mask[n], scores[n] * factor, -1e30)
            top = jnp.maximum(jnp.max(s, axis=1, keepdims=True), f)
            w = jnp.where(mask[n], jnp.exp(s - top), 0.0)
            fw = jnp.exp(f - top)
            whole = jnp.sum(w, axis=1, keepdims=True) + fw
            probs = (w / whole).astype(bf16)
            fp = (fw / whole).astype(bf16).astype(f32)
            mixed = jnp.dot(probs, values[b * kv_heads + g], preferred_element_type=f32)
            mixed = mixed + fp * new_v[n]
            att2d[pl.ds(g * reps * owners + b, reps, stride=owners), :] = mixed
        return carry

    def att_copy(g, d):
        return pltpu.make_async_remote_copy(
            src_ref=att_all.at[g, gx], dst_ref=att_all.at[g, gx], send_sem=as_sem.at[g, d - 1],
            recv_sem=ar_sem.at[g, d - 1], device_id={"gx": lax.rem(gx + d, nx)},
            device_id_type=MESH,
        )

    for g in range(kv_heads):
        lax.fori_loop(0, owners // group, functools.partial(attend, g), 0)
        for h in range(reps):
            at = (g * reps + h) * owners
            att_all[g, gx, :, h * head_dim:(h + 1) * head_dim] = att2d[
                at:at + owners, :
            ].astype(bf16)
        for d in range(1, nx):
            att_copy(g, d).start()
    for ch in range(q_chunks + 1):
        for d in range(1, nx):
            part_copy(ch, d).wait_send()
    for j in range(ny):
        for h in range(halves):
            wo_copy(j, h).wait()
    for g in range(kv_heads):
        for d in range(1, nx):
            att_copy(g, d).wait()
    width = reps * head_dim
    attended = [att_all[g].reshape(batch, width) for g in range(kv_heads)]

    def pair_copy(e, h):
        return pltpu.make_async_remote_copy(
            src_ref=term.at[e, 0, h], dst_ref=pair_in.at[e, h], send_sem=ts_sem.at[e, h],
            recv_sem=tr_sem.at[e, h], device_id={"gy": buddy}, device_id_type=MESH,
        )

    def cross_copy(e, h):
        return pltpu.make_async_remote_copy(
            src_ref=term.at[e, 1, h], dst_ref=cross_in.at[e - 1, h], send_sem=xs_sem.at[e - 1, h],
            recv_sem=xr_sem.at[e - 1, h], device_id={"gy": across(e)}, device_id_type=MESH,
        )

    def out_piece(to, h):
        total = jnp.zeros((batch, CHUNK), f32)
        for g in range(kv_heads):
            at = h * wo_rows + g * width
            total = total + jnp.dot(
                attended[g], wbuf[to, at:at + width, :], preferred_element_type=f32
            )
        return total

    for e in list(range(1, chips)) + [0]:
        there = lax.rem(chip + e, chips) * 2
        for h in range(halves):
            term[e, 0, h] = out_piece(there + 1 - core, h)
            pair_copy(e, h).start()
        for h in range(halves):
            total = out_piece(there + core, h)
            if e > 0:
                pair_copy(e, h).wait_recv()
                term[e, 1, h] = total + pair_in[e, h]
                cross_copy(e, h).start()
            else:
                term[e, 1, h] = total
    for h in range(halves):
        pair_copy(0, h).wait_recv()
        total = term[0, 1, h] + pair_in[0, h]
        for e in range(1, chips):
            cross_copy(e, h).wait_recv()
            total = total + cross_in[e - 1, h]
        out_ref[:, h * CHUNK:(h + 1) * CHUNK] = total.astype(bf16)
    for h in range(halves):
        for e in range(chips):
            pair_copy(e, h).wait_send()
        for e in range(1, chips):
            cross_copy(e, h).wait_send()


def direct_body(
    nx, ny, hidden_in, exponents, signs, lengths, w_query, key_value_weight, w_out,
    keys_cache, cached_value_rows,
):
    batch, feat = hidden_in.shape
    depth, q_cols = w_query.shape
    kv_heads, head_dim = key_value_weight.shape[1], key_value_weight.shape[3]
    owners = batch // nx
    heads = q_cols // head_dim
    reps = heads // kv_heads
    slots = keys_cache.shape[2]
    out_cols = w_out.shape[1]
    parts = 2 * kv_heads
    half = head_dim // 2
    freqs = np.power(500000.0, -(np.arange(half) * 2.0 / head_dim)).astype(np.float32)
    freqs = jnp.asarray(np.concatenate([freqs, freqs])[None, :])
    q_chunks = q_cols // CHUNK
    halves = depth // w_out.shape[0]
    chips = ny // 2
    dims = (batch, feat, q_cols, owners, kv_heads, reps, slots, head_dim, out_cols)
    vmem = pl.BlockSpec(memory_space=pltpu.VMEM)
    anyw = pl.BlockSpec(memory_space=pl.ANY)
    f32, bf16 = jnp.float32, jnp.bfloat16
    dma = pltpu.SemaphoreType.DMA
    lanes = max(batch, 128)
    return pl.pallas_call(
        functools.partial(decode_kernel, nx, ny, dims),
        out_shape=jax.ShapeDtypeStruct((batch, feat), bf16),
        in_specs=[vmem] * 5 + [pl.BlockSpec(memory_space=pltpu.SMEM)] + [anyw] * 5,
        out_specs=vmem,
        scratch_shapes=[
            pltpu.VMEM((q_chunks, depth, CHUNK), bf16),
            pltpu.VMEM((depth * parts, head_dim), bf16),
            pltpu.VMEM((1024, head_dim), f32),
            pltpu.VMEM((depth, parts * head_dim), bf16),
            pltpu.VMEM((owners * kv_heads, slots, head_dim), bf16),
            pltpu.VMEM((owners * kv_heads, slots, head_dim), bf16),
            pltpu.VMEM((ny, batch, feat), bf16),
            pltpu.VMEM((nx * ny, 8, lanes), f32),
            pltpu.VMEM((ny, batch, feat), bf16),
            pltpu.VMEM((q_chunks + 1, nx, owners, CHUNK), f32),
            pltpu.VMEM((q_chunks + 1, nx, owners, CHUNK), f32),
            pltpu.VMEM((heads * owners, head_dim), f32),
            pltpu.VMEM((parts * owners, head_dim), f32),
            pltpu.VMEM((heads * owners, head_dim), f32),
            pltpu.VMEM((kv_heads, nx, owners, reps * head_dim), bf16),
            pltpu.VMEM((chips, 2, halves, batch, CHUNK), f32),
            pltpu.VMEM((chips, halves, batch, CHUNK), f32),
            pltpu.VMEM((chips - 1, halves, batch, CHUNK), f32),
            dma((q_chunks,)), dma, dma, dma, dma((ny, halves)),
            dma((ny - 1,)), dma((ny - 1,)),
            dma((nx * ny - 1,)), dma((nx * ny - 1,)),
            dma((q_chunks + 1, nx - 1)), dma((q_chunks + 1, nx - 1)),
            dma((kv_heads, nx - 1)), dma((kv_heads, nx - 1)),
            dma((chips, halves)), dma((chips, halves)),
            dma((chips - 1, halves)), dma((chips - 1, halves)),
        ],
        compiler_params=pltpu.CompilerParams(
            collective_id=0, has_side_effects=True, vmem_limit_bytes=56 * 1024 * 1024
        ),
    )(
        hidden_in, exponents.T, signs.reshape(1, -1), freqs, lengths.reshape(1, -1), lengths,
        w_query, key_value_weight.reshape(-1, head_dim), w_out,
        keys_cache.reshape(-1, slots, head_dim), cached_value_rows.reshape(-1, slots, head_dim),
    )


def hadamard_table(block_len):
    index_vals = jnp.arange(block_len, dtype=jnp.int32)
    parity = jnp.zeros((block_len, block_len), jnp.int32)
    for bit_number in range(block_len.bit_length() - 1):
        step_size = 2**bit_number
        parity = parity + index_vals[:, None] // step_size % 2 * (
            index_vals[None, :] // step_size % 2
        )
    return jnp.where(parity % 2 == 0, 1.0, -1.0).astype(jnp.float32) / math.sqrt(block_len)


def quantize(blocks, exps, table, signs):
    signed = blocks * (2.0 * signs.astype(jnp.float32) - 1.0)
    rotated = jnp.einsum("bnk,kj->bnj", signed, table, precision=lax.Precision.HIGHEST)
    factor = jnp.exp2(exps.astype(jnp.float32))[..., None]
    coded = jnp.clip(rotated / factor, -4.0, 4.0).astype(jnp.bfloat16)
    return (coded.astype(jnp.float32) * factor).astype(jnp.bfloat16)


def rotary_angles(values, positions):
    half_width = values.shape[-1] // 2
    freqs = jnp.power(
        500000.0, -(jnp.arange(half_width, dtype=jnp.float32) * 2.0 / values.shape[-1])
    )
    angles = positions.astype(jnp.float32).reshape((-1,) + (1,) * (values.ndim - 1)) * freqs
    cosine = jnp.cos(angles)
    sine = jnp.sin(angles)
    first_half = values[..., :half_width]
    second_half = values[..., half_width:]
    return jnp.concatenate(
        [first_half * cosine - second_half * sine, second_half * cosine + first_half * sine],
        axis=-1,
    )


def body(
    hidden_in,
    exponents,
    signs,
    lengths,
    w_query,
    key_value_weight,
    w_out,
    keys_cache,
    cached_value_rows,
):
    batch_all, local_feat = hidden_in.shape
    block_len = signs.shape[0]
    table = hadamard_table(block_len)
    widened = hidden_in.astype(jnp.float32)
    energy = lax.psum(jnp.sum(widened * widened, axis=1, keepdims=True), ("gx", "gy"))
    row_scale = lax.rsqrt(energy / MODEL_WIDTH + 1e-05)
    own_blocks = local_feat // block_len
    own_exps = lax.dynamic_slice_in_dim(exponents, lax.axis_index("gy") * own_blocks, own_blocks, 1)
    coded_own = quantize(
        (widened * row_scale).reshape(batch_all, own_blocks, block_len), own_exps, table, signs
    )
    gathered = lax.all_gather(coded_own.reshape(batch_all, local_feat), "gy", axis=1, tiled=True)
    query_cols = w_query.shape[1]
    kv_heads = key_value_weight.shape[1]
    head_dim = key_value_weight.shape[3]
    kv_flat = key_value_weight.reshape(key_value_weight.shape[0], kv_heads * 2 * head_dim)
    owners = batch_all // lax.axis_size("gx")
    partial_cols = lax.psum_scatter(
        jnp.concatenate(
            [
                jnp.dot(gathered, w_query, preferred_element_type=jnp.float32),
                jnp.dot(gathered, kv_flat, preferred_element_type=jnp.float32),
            ],
            axis=1,
        ),
        "gx",
        scatter_dimension=1,
        tiled=True,
    )
    mine = lax.all_to_all(partial_cols, "gx", split_axis=0, concat_axis=1, tiled=True)
    query_unrotated = mine[:, :query_cols].reshape(owners, kv_heads, -1, head_dim)
    key_value_unrotated = mine[:, query_cols:].reshape(owners, kv_heads, 2, head_dim)
    query_rotated = rotary_angles(query_unrotated, lengths).astype(jnp.bfloat16)
    key_new = rotary_angles(key_value_unrotated[:, :, 0], lengths).astype(jnp.bfloat16)
    value_new = key_value_unrotated[:, :, 1].astype(jnp.bfloat16)
    scale = 1.0 / math.sqrt(head_dim)
    scores = (
        jnp.einsum("bgrd,bgpd->bgrp", query_rotated, keys_cache, preferred_element_type=jnp.float32)
        * scale
    )
    fresh = (
        jnp.einsum("bgrd,bgd->bgr", query_rotated, key_new, preferred_element_type=jnp.float32)
        * scale
    )
    valid = (jnp.arange(keys_cache.shape[2], dtype=jnp.int32)[None, :] < lengths[:, None])[
        :, None, None, :
    ]
    masked = jnp.where(valid, scores, -1e30)
    top = jnp.maximum(jnp.max(masked, axis=-1), fresh)
    weights = jnp.where(valid, jnp.exp(masked - top[..., None]), 0.0)
    fresh_w = jnp.exp(fresh - top)
    total = jnp.sum(weights, axis=-1) + fresh_w
    probs = (weights / total[..., None]).astype(jnp.bfloat16)
    fresh_p = (fresh_w / total).astype(jnp.bfloat16)
    mixed = jnp.einsum(
        "bgrp,bgpd->bgrd", probs, cached_value_rows, preferred_element_type=jnp.float32
    )
    mixed = (
        mixed
        + fresh_p.astype(jnp.float32)[..., None] * value_new.astype(jnp.float32)[:, :, None, :]
    )
    attended = mixed.astype(jnp.bfloat16).reshape(owners, -1)
    terms = jnp.dot(
        lax.all_gather(attended, "gx", axis=0, tiled=True),
        w_out,
        preferred_element_type=jnp.float32,
    )
    summed = lax.psum_scatter(terms, "gy", scatter_dimension=1, tiled=True)
    return summed.astype(jnp.bfloat16)


def solution(mesh):
    in_specs = (
        P("group", ("gx", "gy")),
        P("group", "gx"),
        P(),
        P(("group", "gx")),
        P("gx", "gy"),
        P("gx", "gy", None, None),
        P("gy", "gx"),
        P(("group", "gx"), "gy", None, None),
        P(("group", "gx"), "gy", None, None),
    )
    out_specs = P("group", ("gx", "gy"))
    nx, ny = mesh.shape["gx"], mesh.shape["gy"]
    run = functools.partial(direct_body, nx, ny) if nx * ny <= 16 else body
    return jax.shard_map(run, mesh=mesh, in_specs=in_specs, out_specs=out_specs, check_vma=False)
```

```python
import functools
import math

import jax
import jax.numpy as jnp
import numpy as np
from jax import lax
from jax.experimental import pallas as pl
from jax.experimental.pallas import tpu as pltpu
from jax.sharding import PartitionSpec as P

MODEL_WIDTH = 16384
MESH = pl.DeviceIdType.MESH
CHUNK = 512


def decode_kernel(
    nx, ny, dims,
    hidden_ref, exps_ref, signs_ref, freq_ref, len_row_ref, len_ref,
    wq_hbm, kv_hbm, wout_hbm, keys_hbm, values_hbm,
    out_ref,
    wbuf, kv_raw, kv_stage, kv_w, keys, values,
    hid, en, dec, part, got, q2d, kv2d, att2d, att_all, term, pair_in, cross_in,
    w_sem, kv_sem, k_sem, v_sem, wo_sem,
    hs_sem, hr_sem, es_sem, er_sem, ps_sem, pr_sem, as_sem, ar_sem,
    ts_sem, tr_sem, xs_sem, xr_sem,
):
    batch, feat, q_cols, owners, kv_heads, reps, slots, head_dim, out_cols = dims
    gx = lax.axis_index("gx")
    gy = lax.axis_index("gy")
    peers = nx * ny
    chips = ny // 2
    chip, core = gy // 2, lax.rem(gy, 2)
    buddy = chip * 2 + 1 - core
    me = gx * ny + gy
    block = head_dim
    q_chunks = q_cols // CHUNK
    depth = feat * ny
    heads = kv_heads * reps
    f32, bf16 = jnp.float32, jnp.bfloat16

    barrier = pltpu.get_barrier_semaphore()

    def peer(k):
        idx = lax.rem(me + k, peers)
        return {"gx": idx // ny, "gy": lax.rem(idx, ny)}

    def greet(k, carry):
        pl.semaphore_signal(barrier, inc=1, device_id=peer(k), device_id_type=MESH)
        return carry

    lax.fori_loop(1, peers, greet, 0)

    def kv_copy():
        return pltpu.make_async_copy(kv_hbm, kv_raw, kv_sem)

    def wq_copy(c):
        return pltpu.make_async_copy(
            wq_hbm.at[:, pl.ds(pl.multiple_of(c * CHUNK, CHUNK), CHUNK)], wbuf.at[c], w_sem.at[c]
        )

    kv_copy().start()
    for c in range(q_chunks):
        wq_copy(c).start()
    k_copy = pltpu.make_async_copy(keys_hbm, keys, k_sem)
    v_copy = pltpu.make_async_copy(values_hbm, values, v_sem)

    own = hidden_ref[...]
    wide = own.astype(f32)
    square = wide * wide
    high = square.astype(bf16)
    low = (square - high.astype(f32)).astype(bf16)
    ones = jnp.ones((8, feat), bf16)
    contract = (((1,), (1,)), ((), ()))
    row = lax.dot_general(ones, high, contract, preferred_element_type=f32) + lax.dot_general(
        ones, low, contract, preferred_element_type=f32
    )
    lanes = en.shape[2]
    if lanes > batch:
        row = jnp.concatenate([row, jnp.zeros((8, lanes - batch), f32)], axis=1)
    en[me] = row
    hid[gy] = own

    pl.semaphore_wait(barrier, peers - 1)

    def energy_copy(k):
        return pltpu.make_async_remote_copy(
            src_ref=en.at[me], dst_ref=en.at[me], send_sem=es_sem.at[k - 1],
            recv_sem=er_sem.at[k - 1], device_id=peer(k), device_id_type=MESH,
        )

    def send_energy(k, carry):
        energy_copy(k).start()
        return carry

    def across(e):
        return lax.rem(chip + e, chips) * 2 + core

    def hidden_copy(n):
        src = gy if n < chips else lax.rem(chip + chips - (n - chips + 1), chips) * 2 + core
        to = across(n) if 1 <= n < chips else buddy
        return pltpu.make_async_remote_copy(
            src_ref=hid.at[src], dst_ref=hid.at[src], send_sem=hs_sem.at[n],
            recv_sem=hr_sem.at[n], device_id={"gy": to}, device_id_type=MESH,
        )

    for e in range(1, chips):
        hidden_copy(e).start()
    lax.fori_loop(1, peers, send_energy, 0)
    hidden_copy(0).start()

    lr = lax.broadcasted_iota(jnp.int32, (owners, owners), 0)
    lc = lax.broadcasted_iota(jnp.int32, (owners, owners), 1)
    place = jnp.sum(
        jnp.where(lr == lc, len_row_ref[...].astype(f32), 0.0), axis=1, keepdims=True
    )
    angles = place * freq_ref[...]
    first = lax.broadcasted_iota(jnp.int32, (owners, head_dim), 1) < head_dim // 2
    cosine = jnp.cos(angles)
    sine = jnp.where(first, -1.0, 1.0) * jnp.sin(angles)

    kv_copy().wait()
    parts = kv_heads * 2
    step_rows = kv_stage.shape[0]
    rows_out = step_rows // parts

    def separate(i, carry):
        base = pl.multiple_of(i * step_rows, step_rows)
        kv_stage[...] = kv_raw[pl.ds(base, step_rows), :].astype(f32)
        to = pl.multiple_of(i * rows_out, rows_out)
        for j in range(parts):
            kv_w[pl.ds(to, rows_out), j * head_dim:(j + 1) * head_dim] = kv_stage[
                pl.ds(j, rows_out, stride=parts), :
            ].astype(bf16)
        return carry

    lax.fori_loop(0, depth // rows_out, separate, 0)

    r = lax.broadcasted_iota(jnp.int32, (block, block), 0)
    c = lax.broadcasted_iota(jnp.int32, (block, block), 1)
    common = r & c
    parity = jnp.zeros((block, block), jnp.int32)
    for bit in range(block.bit_length() - 1):
        parity = parity + ((common >> bit) & 1)
    sign_row = 2.0 * signs_ref[...].astype(f32) - 1.0
    sign_col = jnp.sum(jnp.where(r == c, sign_row, 0.0), axis=1, keepdims=True)
    table = (jnp.where((parity & 1) == 0, 1.0, -1.0) * sign_col).astype(bf16)

    for e in range(1, chips):
        hidden_copy(e).wait_recv()
        hidden_copy(chips - 1 + e).start()

    def wait_energy(k, carry):
        energy_copy(k).wait()
        return carry

    lax.fori_loop(1, peers, wait_energy, 0)
    energy_row = jnp.sum(en[...], axis=0)[0:1, :]
    er = lax.broadcasted_iota(jnp.int32, (batch, lanes), 0)
    ec = lax.broadcasted_iota(jnp.int32, (batch, lanes), 1)
    energy = jnp.sum(jnp.where(er == ec, energy_row, 0.0), axis=1, keepdims=True)
    scale_col = lax.rsqrt(energy / MODEL_WIDTH + 1e-05) * (1.0 / math.sqrt(block))
    k_copy.start()
    v_copy.start()
    blocks_each = feat // block
    own_lane = lax.broadcasted_iota(jnp.int32, (batch, batch), 0) == lax.broadcasted_iota(
        jnp.int32, (batch, batch), 1
    )

    def code(src):
        for b in range(blocks_each):
            n = src * blocks_each + b
            exps = exps_ref[pl.ds(n, 1), :]
            factors = jnp.where(
                exps >= 0, jnp.where(exps >= 1, 2.0, 1.0), jnp.where(exps >= -1, 0.5, 0.25)
            )
            factor = jnp.sum(jnp.where(own_lane, factors, 0.0), axis=1, keepdims=True)
            inverse = 1.0 / factor
            raw = jnp.dot(
                hid[src, :, b * block:(b + 1) * block], table, preferred_element_type=f32
            )
            coded = jnp.clip(raw * scale_col * inverse, -4.0, 4.0).astype(bf16)
            dec[src, :, b * block:(b + 1) * block] = (coded.astype(f32) * factor).astype(bf16)

    code(gy)
    for e in range(1, chips):
        code(lax.rem(chip + chips - e, chips) * 2 + core)
    hidden_copy(0).wait_recv()
    code(buddy)
    for e in range(1, chips):
        hidden_copy(chips - 1 + e).wait_recv()
        code(lax.rem(chip + chips - e, chips) * 2 + 1 - core)
    for n in range(ny - 1):
        hidden_copy(n).wait_send()

    def part_copy(ch, d):
        to = lax.rem(gx + d, nx)
        return pltpu.make_async_remote_copy(
            src_ref=part.at[ch, to], dst_ref=got.at[ch, gx], send_sem=ps_sem.at[ch, d - 1],
            recv_sem=pr_sem.at[ch, d - 1], device_id={"gx": to}, device_id_type=MESH,
        )

    def ship(ch, total):
        for j in range(nx):
            part[ch, j] = total[j * owners:(j + 1) * owners]
        for d in range(1, nx):
            part_copy(ch, d).start()

    def project(read):
        total = jnp.zeros((batch, CHUNK), f32)
        for s in range(ny):
            total = total + jnp.dot(dec[s], read(s), preferred_element_type=f32)
        return total

    ship(q_chunks, project(lambda s: kv_w[s * feat:(s + 1) * feat, :]))

    def q_step(ch, carry):
        wq_copy(ch).wait()
        ship(ch, project(lambda s: wbuf[ch, s * feat:(s + 1) * feat, :]))
        return carry

    lax.fori_loop(0, q_chunks, q_step, 0)

    wo_rows = wout_hbm.shape[0]
    halves = depth // wo_rows
    wo_wide = halves * CHUNK

    def wo_copy(j, h):
        return pltpu.make_async_copy(
            wout_hbm.at[:, pl.ds(pl.multiple_of(j * wo_wide + h * CHUNK, CHUNK), CHUNK)],
            wbuf.at[j, pl.ds(h * wo_rows, wo_rows)],
            wo_sem.at[j, h],
        )

    for j in range(ny):
        for h in range(halves):
            wo_copy(j, h).start()

    def rope(v):
        return v * cosine + pltpu.roll(v, head_dim // 2, 1) * sine

    def arrived(ch):
        for d in range(1, nx):
            part_copy(ch, d).wait_recv()
        total = part[ch, gx]
        for d in range(1, nx):
            total = total + got[ch, lax.rem(gx + d, nx)]
        return total

    per = CHUNK // head_dim
    total = arrived(q_chunks)
    for j in range(parts):
        v = total[:, j * head_dim:(j + 1) * head_dim]
        if j % 2 == 0:
            v = rope(v)
        kv2d[j * owners:(j + 1) * owners, :] = v.astype(bf16).astype(f32)

    def take(ch):
        total = arrived(ch)
        for j in range(per):
            h = ch * per + j
            v = rope(total[:, j * head_dim:(j + 1) * head_dim])
            q2d[h * owners:(h + 1) * owners, :] = v.astype(bf16).astype(f32)

    taken = 0
    k_copy.wait()
    v_copy.wait()
    factor = 1.0 / math.sqrt(head_dim)
    position = lax.broadcasted_iota(jnp.int32, (reps, slots), 1)
    group = 8

    def attend(g, i, carry):
        scores, fresh, mask, new_v = [], [], [], []
        for jb in range(group):
            b = i * group + jb
            q = q2d[pl.ds(g * reps * owners + b, reps, stride=owners), :]
            k_new = kv2d[pl.ds(2 * g * owners + b, 1), :]
            new_v.append(kv2d[pl.ds((2 * g + 1) * owners + b, 1), :])
            scores.append(
                lax.dot_general(
                    q.astype(bf16), keys[b * kv_heads + g], contract, preferred_element_type=f32
                )
            )
            fresh.append(jnp.sum(q * k_new, axis=1, keepdims=True))
            mask.append(position < len_ref[b])
        for n in range(group):
            b = i * group + n
            f = fresh[n] * factor
            s = jnp.where(mask[n], scores[n] * factor, -1e30)
            top = jnp.maximum(jnp.max(s, axis=1, keepdims=True), f)
            w = jnp.where(mask[n], jnp.exp(s - top), 0.0)
            fw = jnp.exp(f - top)
            whole = jnp.sum(w, axis=1, keepdims=True) + fw
            probs = (w / whole).astype(bf16)
            fp = (fw / whole).astype(bf16).astype(f32)
            mixed = jnp.dot(probs, values[b * kv_heads + g], preferred_element_type=f32)
            mixed = mixed + fp * new_v[n]
            att2d[pl.ds(g * reps * owners + b, reps, stride=owners), :] = mixed
        return carry

    def att_copy(g, d):
        return pltpu.make_async_remote_copy(
            src_ref=att_all.at[g, gx], dst_ref=att_all.at[g, gx], send_sem=as_sem.at[g, d - 1],
            recv_sem=ar_sem.at[g, d - 1], device_id={"gx": lax.rem(gx + d, nx)},
            device_id_type=MESH,
        )

    for g in range(kv_heads):
        while taken < q_chunks and taken * per < (g + 1) * reps:
            take(taken)
            taken += 1
        lax.fori_loop(0, owners // group, functools.partial(attend, g), 0)
        for h in range(reps):
            at = (g * reps + h) * owners
            att_all[g, gx, :, h * head_dim:(h + 1) * head_dim] = att2d[
                at:at + owners, :
            ].astype(bf16)
        for d in range(1, nx):
            att_copy(g, d).start()
    for ch in range(q_chunks + 1):
        for d in range(1, nx):
            part_copy(ch, d).wait_send()
    for j in range(ny):
        for h in range(halves):
            wo_copy(j, h).wait()
    width = reps * head_dim

    def out_piece(to, h, g):
        at = h * wo_rows + g * width
        return jnp.dot(
            att_all[g].reshape(batch, width), wbuf[to, at:at + width, :],
            preferred_element_type=f32,
        )

    def place_of(e, role):
        return lax.rem(chip + e, chips) * 2 + (core if role else 1 - core)

    for g in range(kv_heads):
        for d in range(1, nx):
            att_copy(g, d).wait()
        if g == kv_heads - 1:
            break
        for e in range(chips):
            for role in range(2):
                for h in range(halves):
                    piece = out_piece(place_of(e, role), h, g)
                    term[e, role, h] = piece if g == 0 else term[e, role, h] + piece

    def finish(e, role, h):
        piece = out_piece(place_of(e, role), h, kv_heads - 1)
        return piece if kv_heads == 1 else term[e, role, h] + piece

    def pair_copy(e, h):
        return pltpu.make_async_remote_copy(
            src_ref=term.at[e, 0, h], dst_ref=pair_in.at[e, h], send_sem=ts_sem.at[e, h],
            recv_sem=tr_sem.at[e, h], device_id={"gy": buddy}, device_id_type=MESH,
        )

    def cross_copy(e, h):
        return pltpu.make_async_remote_copy(
            src_ref=term.at[e, 1, h], dst_ref=cross_in.at[e - 1, h], send_sem=xs_sem.at[e - 1, h],
            recv_sem=xr_sem.at[e - 1, h], device_id={"gy": across(e)}, device_id_type=MESH,
        )

    for e in list(range(1, chips)) + [0]:
        for h in range(halves):
            term[e, 0, h] = finish(e, 0, h)
            pair_copy(e, h).start()
        for h in range(halves):
            total = finish(e, 1, h)
            if e > 0:
                pair_copy(e, h).wait_recv()
                term[e, 1, h] = total + pair_in[e, h]
                cross_copy(e, h).start()
            else:
                term[e, 1, h] = total
    for h in range(halves):
        pair_copy(0, h).wait_recv()
        total = term[0, 1, h] + pair_in[0, h]
        for e in range(1, chips):
            cross_copy(e, h).wait_recv()
            total = total + cross_in[e - 1, h]
        out_ref[:, h * CHUNK:(h + 1) * CHUNK] = total.astype(bf16)
    for h in range(halves):
        for e in range(chips):
            pair_copy(e, h).wait_send()
        for e in range(1, chips):
            cross_copy(e, h).wait_send()


def direct_body(
    nx, ny, hidden_in, exponents, signs, lengths, w_query, key_value_weight, w_out,
    keys_cache, cached_value_rows,
):
    batch, feat = hidden_in.shape
    depth, q_cols = w_query.shape
    kv_heads, head_dim = key_value_weight.shape[1], key_value_weight.shape[3]
    owners = batch // nx
    heads = q_cols // head_dim
    reps = heads // kv_heads
    slots = keys_cache.shape[2]
    out_cols = w_out.shape[1]
    parts = 2 * kv_heads
    half = head_dim // 2
    freqs = np.power(500000.0, -(np.arange(half) * 2.0 / head_dim)).astype(np.float32)
    freqs = jnp.asarray(np.concatenate([freqs, freqs])[None, :])
    q_chunks = q_cols // CHUNK
    halves = depth // w_out.shape[0]
    chips = ny // 2
    dims = (batch, feat, q_cols, owners, kv_heads, reps, slots, head_dim, out_cols)
    vmem = pl.BlockSpec(memory_space=pltpu.VMEM)
    anyw = pl.BlockSpec(memory_space=pl.ANY)
    f32, bf16 = jnp.float32, jnp.bfloat16
    dma = pltpu.SemaphoreType.DMA
    lanes = max(batch, 128)
    return pl.pallas_call(
        functools.partial(decode_kernel, nx, ny, dims),
        out_shape=jax.ShapeDtypeStruct((batch, feat), bf16),
        in_specs=[vmem] * 5 + [pl.BlockSpec(memory_space=pltpu.SMEM)] + [anyw] * 5,
        out_specs=vmem,
        scratch_shapes=[
            pltpu.VMEM((q_chunks, depth, CHUNK), bf16),
            pltpu.VMEM((depth * parts, head_dim), bf16),
            pltpu.VMEM((1024, head_dim), f32),
            pltpu.VMEM((depth, parts * head_dim), bf16),
            pltpu.VMEM((owners * kv_heads, slots, head_dim), bf16),
            pltpu.VMEM((owners * kv_heads, slots, head_dim), bf16),
            pltpu.VMEM((ny, batch, feat), bf16),
            pltpu.VMEM((nx * ny, 8, lanes), f32),
            pltpu.VMEM((ny, batch, feat), bf16),
            pltpu.VMEM((q_chunks + 1, nx, owners, CHUNK), f32),
            pltpu.VMEM((q_chunks + 1, nx, owners, CHUNK), f32),
            pltpu.VMEM((heads * owners, head_dim), f32),
            pltpu.VMEM((parts * owners, head_dim), f32),
            pltpu.VMEM((heads * owners, head_dim), f32),
            pltpu.VMEM((kv_heads, nx, owners, reps * head_dim), bf16),
            pltpu.VMEM((chips, 2, halves, batch, CHUNK), f32),
            pltpu.VMEM((chips, halves, batch, CHUNK), f32),
            pltpu.VMEM((chips - 1, halves, batch, CHUNK), f32),
            dma((q_chunks,)), dma, dma, dma, dma((ny, halves)),
            dma((ny - 1,)), dma((ny - 1,)),
            dma((nx * ny - 1,)), dma((nx * ny - 1,)),
            dma((q_chunks + 1, nx - 1)), dma((q_chunks + 1, nx - 1)),
            dma((kv_heads, nx - 1)), dma((kv_heads, nx - 1)),
            dma((chips, halves)), dma((chips, halves)),
            dma((chips - 1, halves)), dma((chips - 1, halves)),
        ],
        compiler_params=pltpu.CompilerParams(
            collective_id=0, has_side_effects=True, vmem_limit_bytes=56 * 1024 * 1024
        ),
    )(
        hidden_in, exponents.T, signs.reshape(1, -1), freqs, lengths.reshape(1, -1), lengths,
        w_query, key_value_weight.reshape(-1, head_dim), w_out,
        keys_cache.reshape(-1, slots, head_dim), cached_value_rows.reshape(-1, slots, head_dim),
    )


def hadamard_table(block_len):
    index_vals = jnp.arange(block_len, dtype=jnp.int32)
    parity = jnp.zeros((block_len, block_len), jnp.int32)
    for bit_number in range(block_len.bit_length() - 1):
        step_size = 2**bit_number
        parity = parity + index_vals[:, None] // step_size % 2 * (
            index_vals[None, :] // step_size % 2
        )
    return jnp.where(parity % 2 == 0, 1.0, -1.0).astype(jnp.float32) / math.sqrt(block_len)


def quantize(blocks, exps, table, signs):
    signed = blocks * (2.0 * signs.astype(jnp.float32) - 1.0)
    rotated = jnp.einsum("bnk,kj->bnj", signed, table, precision=lax.Precision.HIGHEST)
    factor = jnp.exp2(exps.astype(jnp.float32))[..., None]
    coded = jnp.clip(rotated / factor, -4.0, 4.0).astype(jnp.bfloat16)
    return (coded.astype(jnp.float32) * factor).astype(jnp.bfloat16)


def rotary_angles(values, positions):
    half_width = values.shape[-1] // 2
    freqs = jnp.power(
        500000.0, -(jnp.arange(half_width, dtype=jnp.float32) * 2.0 / values.shape[-1])
    )
    angles = positions.astype(jnp.float32).reshape((-1,) + (1,) * (values.ndim - 1)) * freqs
    cosine = jnp.cos(angles)
    sine = jnp.sin(angles)
    first_half = values[..., :half_width]
    second_half = values[..., half_width:]
    return jnp.concatenate(
        [first_half * cosine - second_half * sine, second_half * cosine + first_half * sine],
        axis=-1,
    )


def body(
    hidden_in,
    exponents,
    signs,
    lengths,
    w_query,
    key_value_weight,
    w_out,
    keys_cache,
    cached_value_rows,
):
    batch_all, local_feat = hidden_in.shape
    block_len = signs.shape[0]
    table = hadamard_table(block_len)
    widened = hidden_in.astype(jnp.float32)
    energy = lax.psum(jnp.sum(widened * widened, axis=1, keepdims=True), ("gx", "gy"))
    row_scale = lax.rsqrt(energy / MODEL_WIDTH + 1e-05)
    own_blocks = local_feat // block_len
    own_exps = lax.dynamic_slice_in_dim(exponents, lax.axis_index("gy") * own_blocks, own_blocks, 1)
    coded_own = quantize(
        (widened * row_scale).reshape(batch_all, own_blocks, block_len), own_exps, table, signs
    )
    gathered = lax.all_gather(coded_own.reshape(batch_all, local_feat), "gy", axis=1, tiled=True)
    query_cols = w_query.shape[1]
    kv_heads = key_value_weight.shape[1]
    head_dim = key_value_weight.shape[3]
    kv_flat = key_value_weight.reshape(key_value_weight.shape[0], kv_heads * 2 * head_dim)
    owners = batch_all // lax.axis_size("gx")
    partial_cols = lax.psum_scatter(
        jnp.concatenate(
            [
                jnp.dot(gathered, w_query, preferred_element_type=jnp.float32),
                jnp.dot(gathered, kv_flat, preferred_element_type=jnp.float32),
            ],
            axis=1,
        ),
        "gx",
        scatter_dimension=1,
        tiled=True,
    )
    mine = lax.all_to_all(partial_cols, "gx", split_axis=0, concat_axis=1, tiled=True)
    query_unrotated = mine[:, :query_cols].reshape(owners, kv_heads, -1, head_dim)
    key_value_unrotated = mine[:, query_cols:].reshape(owners, kv_heads, 2, head_dim)
    query_rotated = rotary_angles(query_unrotated, lengths).astype(jnp.bfloat16)
    key_new = rotary_angles(key_value_unrotated[:, :, 0], lengths).astype(jnp.bfloat16)
    value_new = key_value_unrotated[:, :, 1].astype(jnp.bfloat16)
    scale = 1.0 / math.sqrt(head_dim)
    scores = (
        jnp.einsum("bgrd,bgpd->bgrp", query_rotated, keys_cache, preferred_element_type=jnp.float32)
        * scale
    )
    fresh = (
        jnp.einsum("bgrd,bgd->bgr", query_rotated, key_new, preferred_element_type=jnp.float32)
        * scale
    )
    valid = (jnp.arange(keys_cache.shape[2], dtype=jnp.int32)[None, :] < lengths[:, None])[
        :, None, None, :
    ]
    masked = jnp.where(valid, scores, -1e30)
    top = jnp.maximum(jnp.max(masked, axis=-1), fresh)
    weights = jnp.where(valid, jnp.exp(masked - top[..., None]), 0.0)
    fresh_w = jnp.exp(fresh - top)
    total = jnp.sum(weights, axis=-1) + fresh_w
    probs = (weights / total[..., None]).astype(jnp.bfloat16)
    fresh_p = (fresh_w / total).astype(jnp.bfloat16)
    mixed = jnp.einsum(
        "bgrp,bgpd->bgrd", probs, cached_value_rows, preferred_element_type=jnp.float32
    )
    mixed = (
        mixed
        + fresh_p.astype(jnp.float32)[..., None] * value_new.astype(jnp.float32)[:, :, None, :]
    )
    attended = mixed.astype(jnp.bfloat16).reshape(owners, -1)
    terms = jnp.dot(
        lax.all_gather(attended, "gx", axis=0, tiled=True),
        w_out,
        preferred_element_type=jnp.float32,
    )
    summed = lax.psum_scatter(terms, "gy", scatter_dimension=1, tiled=True)
    return summed.astype(jnp.bfloat16)


def solution(mesh):
    in_specs = (
        P("group", ("gx", "gy")),
        P("group", "gx"),
        P(),
        P(("group", "gx")),
        P("gx", "gy"),
        P("gx", "gy", None, None),
        P("gy", "gx"),
        P(("group", "gx"), "gy", None, None),
        P(("group", "gx"), "gy", None, None),
    )
    out_specs = P("group", ("gx", "gy"))
    nx, ny = mesh.shape["gx"], mesh.shape["gy"]
    run = functools.partial(direct_body, nx, ny) if nx * ny <= 16 else body
    return jax.shard_map(run, mesh=mesh, in_specs=in_specs, out_specs=out_specs, check_vma=False)
```

```python
import functools
import math

import jax
import jax.numpy as jnp
import numpy as np
from jax import lax
from jax.experimental import pallas as pl
from jax.experimental.pallas import tpu as pltpu
from jax.sharding import PartitionSpec as P

MODEL_WIDTH = 16384
MESH = pl.DeviceIdType.MESH
CHUNK = 512


def decode_kernel(
    nx, ny, dims,
    hidden_ref, exps_ref, signs_ref, freq_ref, len_row_ref, len_ref,
    wq_hbm, kv_hbm, wout_hbm, keys_hbm, values_hbm,
    out_ref,
    wbuf, kv_raw, kv_stage, kv_w, keys, values,
    hid, en, scales, dec, part, got, q2d, kv2d, att2d, att_all, term, pair_in, cross_in,
    w_sem, kv_sem, k_sem, v_sem, wo_sem,
    hs_sem, hr_sem, es_sem, er_sem, ps_sem, pr_sem, as_sem, ar_sem,
    ts_sem, tr_sem, xs_sem, xr_sem,
):
    batch, feat, q_cols, owners, kv_heads, reps, slots, head_dim, out_cols = dims
    gx = lax.axis_index("gx")
    gy = lax.axis_index("gy")
    peers = nx * ny
    chips = ny // 2
    chip, core = gy // 2, lax.rem(gy, 2)
    buddy = chip * 2 + 1 - core
    me = gx * ny + gy
    block = head_dim
    q_chunks = q_cols // CHUNK
    depth = feat * ny
    heads = kv_heads * reps
    f32, bf16 = jnp.float32, jnp.bfloat16

    barrier = pltpu.get_barrier_semaphore()

    def peer(k):
        idx = lax.rem(me + k, peers)
        return {"gx": idx // ny, "gy": lax.rem(idx, ny)}

    def greet(k, carry):
        pl.semaphore_signal(barrier, inc=1, device_id=peer(k), device_id_type=MESH)
        return carry

    lax.fori_loop(1, peers, greet, 0)

    def kv_copy():
        return pltpu.make_async_copy(kv_hbm, kv_raw, kv_sem)

    def wq_copy(c):
        return pltpu.make_async_copy(
            wq_hbm.at[:, pl.ds(pl.multiple_of(c * CHUNK, CHUNK), CHUNK)], wbuf.at[c], w_sem.at[c]
        )

    early = min(q_chunks, -(-reps * head_dim // CHUNK))
    for c in range(early):
        wq_copy(c).start()
    kv_copy().start()
    for c in range(early, q_chunks):
        wq_copy(c).start()
    k_copy = pltpu.make_async_copy(keys_hbm, keys, k_sem)
    v_copy = pltpu.make_async_copy(values_hbm, values, v_sem)

    own = hidden_ref[...]
    wide = own.astype(f32)
    square = wide * wide
    high = square.astype(bf16)
    low = (square - high.astype(f32)).astype(bf16)
    ones = jnp.ones((8, feat), bf16)
    contract = (((1,), (1,)), ((), ()))
    row = lax.dot_general(ones, high, contract, preferred_element_type=f32) + lax.dot_general(
        ones, low, contract, preferred_element_type=f32
    )
    lanes = en.shape[2]
    if lanes > batch:
        row = jnp.concatenate([row, jnp.zeros((8, lanes - batch), f32)], axis=1)
    en[me] = row
    hid[gy] = own

    pl.semaphore_wait(barrier, peers - 1)

    def energy_copy(k):
        return pltpu.make_async_remote_copy(
            src_ref=en.at[me], dst_ref=en.at[me], send_sem=es_sem.at[k - 1],
            recv_sem=er_sem.at[k - 1], device_id=peer(k), device_id_type=MESH,
        )

    def send_energy(k, carry):
        energy_copy(k).start()
        return carry

    def across(e):
        return lax.rem(chip + e, chips) * 2 + core

    def hidden_copy(n):
        src = gy if n < chips else lax.rem(chip + chips - (n - chips + 1), chips) * 2 + core
        to = across(n) if 1 <= n < chips else buddy
        return pltpu.make_async_remote_copy(
            src_ref=hid.at[src], dst_ref=hid.at[src], send_sem=hs_sem.at[n],
            recv_sem=hr_sem.at[n], device_id={"gy": to}, device_id_type=MESH,
        )

    for e in range(1, chips):
        hidden_copy(e).start()
    lax.fori_loop(1, peers, send_energy, 0)
    hidden_copy(0).start()

    lr = lax.broadcasted_iota(jnp.int32, (owners, owners), 0)
    lc = lax.broadcasted_iota(jnp.int32, (owners, owners), 1)
    place = jnp.sum(
        jnp.where(lr == lc, len_row_ref[...].astype(f32), 0.0), axis=1, keepdims=True
    )
    angles = place * freq_ref[...]
    first = lax.broadcasted_iota(jnp.int32, (owners, head_dim), 1) < head_dim // 2
    cosine = jnp.cos(angles)
    sine = jnp.where(first, -1.0, 1.0) * jnp.sin(angles)

    r = lax.broadcasted_iota(jnp.int32, (block, block), 0)
    c = lax.broadcasted_iota(jnp.int32, (block, block), 1)
    common = r & c
    parity = jnp.zeros((block, block), jnp.int32)
    for bit in range(block.bit_length() - 1):
        parity = parity + ((common >> bit) & 1)
    sign_row = 2.0 * signs_ref[...].astype(f32) - 1.0
    sign_col = jnp.sum(jnp.where(r == c, sign_row, 0.0), axis=1, keepdims=True)
    table = (jnp.where((parity & 1) == 0, 1.0, -1.0) * sign_col).astype(bf16)

    own_lane = lax.broadcasted_iota(jnp.int32, (batch, batch), 0) == lax.broadcasted_iota(
        jnp.int32, (batch, batch), 1
    )

    def spread(n, carry):
        exps = exps_ref[pl.ds(n, 1), :]
        factors = jnp.where(
            exps >= 0, jnp.where(exps >= 1, 2.0, 1.0), jnp.where(exps >= -1, 0.5, 0.25)
        )
        factor = jnp.sum(jnp.where(own_lane, factors, 0.0), axis=1, keepdims=True)
        scales[n, 0] = jnp.broadcast_to(factor, (batch, block))
        scales[n, 1] = jnp.broadcast_to(1.0 / factor, (batch, block))
        return carry

    lax.fori_loop(0, depth // block, spread, 0)

    for e in range(1, chips):
        hidden_copy(e).wait_recv()
        hidden_copy(chips - 1 + e).start()

    def wait_energy(k, carry):
        energy_copy(k).wait()
        return carry

    lax.fori_loop(1, peers, wait_energy, 0)
    energy_row = jnp.sum(en[...], axis=0)[0:1, :]
    er = lax.broadcasted_iota(jnp.int32, (batch, lanes), 0)
    ec = lax.broadcasted_iota(jnp.int32, (batch, lanes), 1)
    energy = jnp.sum(jnp.where(er == ec, energy_row, 0.0), axis=1, keepdims=True)
    scale_col = lax.rsqrt(energy / MODEL_WIDTH + 1e-05) * (1.0 / math.sqrt(block))
    k_copy.start()
    v_copy.start()
    blocks_each = feat // block
    def code(src):
        for b in range(blocks_each):
            n = src * blocks_each + b
            raw = jnp.dot(
                hid[src, :, b * block:(b + 1) * block], table, preferred_element_type=f32
            )
            coded = jnp.clip(raw * scale_col * scales[n, 1], -4.0, 4.0).astype(bf16)
            dec[src, :, b * block:(b + 1) * block] = (coded.astype(f32) * scales[n, 0]).astype(bf16)

    code(gy)
    for e in range(1, chips):
        code(lax.rem(chip + chips - e, chips) * 2 + core)
    hidden_copy(0).wait_recv()
    code(buddy)
    for e in range(1, chips):
        hidden_copy(chips - 1 + e).wait_recv()
        code(lax.rem(chip + chips - e, chips) * 2 + 1 - core)
    for n in range(ny - 1):
        hidden_copy(n).wait_send()

    def part_copy(ch, d):
        to = lax.rem(gx + d, nx)
        return pltpu.make_async_remote_copy(
            src_ref=part.at[ch, to], dst_ref=got.at[ch, gx], send_sem=ps_sem.at[ch, d - 1],
            recv_sem=pr_sem.at[ch, d - 1], device_id={"gx": to}, device_id_type=MESH,
        )

    def ship(ch, total):
        for j in range(nx):
            part[ch, j] = total[j * owners:(j + 1) * owners]
        for d in range(1, nx):
            part_copy(ch, d).start()

    def project(read):
        total = jnp.zeros((batch, CHUNK), f32)
        for s in range(ny):
            total = total + jnp.dot(dec[s], read(s), preferred_element_type=f32)
        return total

    def q_step(ch, carry):
        wq_copy(ch).wait()
        ship(ch, project(lambda s: wbuf[ch, s * feat:(s + 1) * feat, :]))
        return carry

    lax.fori_loop(0, early, q_step, 0)

    kv_copy().wait()
    parts = kv_heads * 2
    step_rows = kv_stage.shape[0]
    rows_out = step_rows // parts

    def separate(i, carry):
        base = pl.multiple_of(i * step_rows, step_rows)
        kv_stage[...] = kv_raw[pl.ds(base, step_rows), :].astype(f32)
        to = pl.multiple_of(i * rows_out, rows_out)
        for j in range(parts):
            kv_w[pl.ds(to, rows_out), j * head_dim:(j + 1) * head_dim] = kv_stage[
                pl.ds(j, rows_out, stride=parts), :
            ].astype(bf16)
        return carry

    lax.fori_loop(0, depth // rows_out, separate, 0)
    ship(q_chunks, project(lambda s: kv_w[s * feat:(s + 1) * feat, :]))
    lax.fori_loop(early, q_chunks, q_step, 0)

    wo_rows = wout_hbm.shape[0]
    halves = depth // wo_rows
    wo_wide = halves * CHUNK

    def wo_copy(j, h):
        return pltpu.make_async_copy(
            wout_hbm.at[:, pl.ds(pl.multiple_of(j * wo_wide + h * CHUNK, CHUNK), CHUNK)],
            wbuf.at[j, pl.ds(h * wo_rows, wo_rows)],
            wo_sem.at[j, h],
        )

    for j in range(ny):
        for h in range(halves):
            wo_copy(j, h).start()

    def rope(v):
        return v * cosine + pltpu.roll(v, head_dim // 2, 1) * sine

    def arrived(ch):
        for d in range(1, nx):
            part_copy(ch, d).wait_recv()
        total = part[ch, gx]
        for d in range(1, nx):
            total = total + got[ch, lax.rem(gx + d, nx)]
        return total

    per = CHUNK // head_dim
    total = arrived(q_chunks)
    for j in range(parts):
        v = total[:, j * head_dim:(j + 1) * head_dim]
        if j % 2 == 0:
            v = rope(v)
        kv2d[j * owners:(j + 1) * owners, :] = v.astype(bf16).astype(f32)

    def take(ch):
        total = arrived(ch)
        for j in range(per):
            h = ch * per + j
            v = rope(total[:, j * head_dim:(j + 1) * head_dim])
            q2d[h * owners:(h + 1) * owners, :] = v.astype(bf16).astype(f32)

    taken = 0
    k_copy.wait()
    v_copy.wait()
    factor = 1.0 / math.sqrt(head_dim)
    position = lax.broadcasted_iota(jnp.int32, (reps, slots), 1)
    group = 8

    def attend(g, i, carry):
        scores, fresh, mask, new_v = [], [], [], []
        for jb in range(group):
            b = i * group + jb
            q = q2d[pl.ds(g * reps * owners + b, reps, stride=owners), :]
            k_new = kv2d[pl.ds(2 * g * owners + b, 1), :]
            new_v.append(kv2d[pl.ds((2 * g + 1) * owners + b, 1), :])
            scores.append(
                lax.dot_general(
                    q.astype(bf16), keys[b * kv_heads + g], contract, preferred_element_type=f32
                )
            )
            fresh.append(jnp.sum(q * k_new, axis=1, keepdims=True))
            mask.append(position < len_ref[b])
        for n in range(group):
            b = i * group + n
            f = fresh[n] * factor
            s = jnp.where(mask[n], scores[n] * factor, -1e30)
            top = jnp.maximum(jnp.max(s, axis=1, keepdims=True), f)
            w = jnp.exp(s - top)
            fw = jnp.exp(f - top)
            whole = jnp.sum(w, axis=1, keepdims=True) + fw
            probs = (w / whole).astype(bf16)
            fp = (fw / whole).astype(bf16).astype(f32)
            mixed = jnp.dot(probs, values[b * kv_heads + g], preferred_element_type=f32)
            mixed = mixed + fp * new_v[n]
            att2d[pl.ds(g * reps * owners + b, reps, stride=owners), :] = mixed
        return carry

    def att_copy(g, d):
        return pltpu.make_async_remote_copy(
            src_ref=att_all.at[g, gx], dst_ref=att_all.at[g, gx], send_sem=as_sem.at[g, d - 1],
            recv_sem=ar_sem.at[g, d - 1], device_id={"gx": lax.rem(gx + d, nx)},
            device_id_type=MESH,
        )

    for g in range(kv_heads):
        while taken < q_chunks and taken * per < (g + 1) * reps:
            take(taken)
            taken += 1
        lax.fori_loop(0, owners // group, functools.partial(attend, g), 0)
        for h in range(reps):
            at = (g * reps + h) * owners
            att_all[g, gx, :, h * head_dim:(h + 1) * head_dim] = att2d[
                at:at + owners, :
            ].astype(bf16)
        for d in range(1, nx):
            att_copy(g, d).start()
    for ch in range(q_chunks + 1):
        for d in range(1, nx):
            part_copy(ch, d).wait_send()
    for j in range(ny):
        for h in range(halves):
            wo_copy(j, h).wait()
    width = reps * head_dim

    def out_piece(to, h, g):
        at = h * wo_rows + g * width
        return jnp.dot(
            att_all[g].reshape(batch, width), wbuf[to, at:at + width, :],
            preferred_element_type=f32,
        )

    def place_of(e, role):
        return lax.rem(chip + e, chips) * 2 + (core if role else 1 - core)

    for g in range(kv_heads):
        for d in range(1, nx):
            att_copy(g, d).wait()
        if g == kv_heads - 1:
            break
        for e in range(chips):
            for role in range(2):
                for h in range(halves):
                    piece = out_piece(place_of(e, role), h, g)
                    term[e, role, h] = piece if g == 0 else term[e, role, h] + piece

    def finish(e, role, h):
        piece = out_piece(place_of(e, role), h, kv_heads - 1)
        return piece if kv_heads == 1 else term[e, role, h] + piece

    def pair_copy(e, h):
        return pltpu.make_async_remote_copy(
            src_ref=term.at[e, 0, h], dst_ref=pair_in.at[e, h], send_sem=ts_sem.at[e, h],
            recv_sem=tr_sem.at[e, h], device_id={"gy": buddy}, device_id_type=MESH,
        )

    def cross_copy(e, h):
        return pltpu.make_async_remote_copy(
            src_ref=term.at[e, 1, h], dst_ref=cross_in.at[e - 1, h], send_sem=xs_sem.at[e - 1, h],
            recv_sem=xr_sem.at[e - 1, h], device_id={"gy": across(e)}, device_id_type=MESH,
        )

    for e in list(range(1, chips)) + [0]:
        for h in range(halves):
            term[e, 0, h] = finish(e, 0, h)
            pair_copy(e, h).start()
        for h in range(halves):
            total = finish(e, 1, h)
            if e > 0:
                pair_copy(e, h).wait_recv()
                term[e, 1, h] = total + pair_in[e, h]
                cross_copy(e, h).start()
            else:
                term[e, 1, h] = total
    for h in range(halves):
        pair_copy(0, h).wait_recv()
        total = term[0, 1, h] + pair_in[0, h]
        for e in range(1, chips):
            cross_copy(e, h).wait_recv()
            total = total + cross_in[e - 1, h]
        out_ref[:, h * CHUNK:(h + 1) * CHUNK] = total.astype(bf16)
    for h in range(halves):
        for e in range(chips):
            pair_copy(e, h).wait_send()
        for e in range(1, chips):
            cross_copy(e, h).wait_send()


def direct_body(
    nx, ny, hidden_in, exponents, signs, lengths, w_query, key_value_weight, w_out,
    keys_cache, cached_value_rows,
):
    batch, feat = hidden_in.shape
    depth, q_cols = w_query.shape
    kv_heads, head_dim = key_value_weight.shape[1], key_value_weight.shape[3]
    owners = batch // nx
    heads = q_cols // head_dim
    reps = heads // kv_heads
    slots = keys_cache.shape[2]
    out_cols = w_out.shape[1]
    parts = 2 * kv_heads
    half = head_dim // 2
    freqs = np.power(500000.0, -(np.arange(half) * 2.0 / head_dim)).astype(np.float32)
    freqs = jnp.asarray(np.concatenate([freqs, freqs])[None, :])
    q_chunks = q_cols // CHUNK
    halves = depth // w_out.shape[0]
    chips = ny // 2
    dims = (batch, feat, q_cols, owners, kv_heads, reps, slots, head_dim, out_cols)
    vmem = pl.BlockSpec(memory_space=pltpu.VMEM)
    anyw = pl.BlockSpec(memory_space=pl.ANY)
    f32, bf16 = jnp.float32, jnp.bfloat16
    dma = pltpu.SemaphoreType.DMA
    lanes = max(batch, 128)
    return pl.pallas_call(
        functools.partial(decode_kernel, nx, ny, dims),
        out_shape=jax.ShapeDtypeStruct((batch, feat), bf16),
        in_specs=[vmem] * 5 + [pl.BlockSpec(memory_space=pltpu.SMEM)] + [anyw] * 5,
        out_specs=vmem,
        scratch_shapes=[
            pltpu.VMEM((q_chunks, depth, CHUNK), bf16),
            pltpu.VMEM((depth * parts, head_dim), bf16),
            pltpu.VMEM((1024, head_dim), f32),
            pltpu.VMEM((depth, parts * head_dim), bf16),
            pltpu.VMEM((owners * kv_heads, slots, head_dim), bf16),
            pltpu.VMEM((owners * kv_heads, slots, head_dim), bf16),
            pltpu.VMEM((ny, batch, feat), bf16),
            pltpu.VMEM((nx * ny, 8, lanes), f32),
            pltpu.VMEM((depth // signs.shape[0], 2, batch, signs.shape[0]), f32),
            pltpu.VMEM((ny, batch, feat), bf16),
            pltpu.VMEM((q_chunks + 1, nx, owners, CHUNK), f32),
            pltpu.VMEM((q_chunks + 1, nx, owners, CHUNK), f32),
            pltpu.VMEM((heads * owners, head_dim), f32),
            pltpu.VMEM((parts * owners, head_dim), f32),
            pltpu.VMEM((heads * owners, head_dim), f32),
            pltpu.VMEM((kv_heads, nx, owners, reps * head_dim), bf16),
            pltpu.VMEM((chips, 2, halves, batch, CHUNK), f32),
            pltpu.VMEM((chips, halves, batch, CHUNK), f32),
            pltpu.VMEM((chips - 1, halves, batch, CHUNK), f32),
            dma((q_chunks,)), dma, dma, dma, dma((ny, halves)),
            dma((ny - 1,)), dma((ny - 1,)),
            dma((nx * ny - 1,)), dma((nx * ny - 1,)),
            dma((q_chunks + 1, nx - 1)), dma((q_chunks + 1, nx - 1)),
            dma((kv_heads, nx - 1)), dma((kv_heads, nx - 1)),
            dma((chips, halves)), dma((chips, halves)),
            dma((chips - 1, halves)), dma((chips - 1, halves)),
        ],
        compiler_params=pltpu.CompilerParams(
            collective_id=0, has_side_effects=True, vmem_limit_bytes=56 * 1024 * 1024
        ),
    )(
        hidden_in, exponents.T, signs.reshape(1, -1), freqs, lengths.reshape(1, -1), lengths,
        w_query, key_value_weight.reshape(-1, head_dim), w_out,
        keys_cache.reshape(-1, slots, head_dim), cached_value_rows.reshape(-1, slots, head_dim),
    )


def hadamard_table(block_len):
    index_vals = jnp.arange(block_len, dtype=jnp.int32)
    parity = jnp.zeros((block_len, block_len), jnp.int32)
    for bit_number in range(block_len.bit_length() - 1):
        step_size = 2**bit_number
        parity = parity + index_vals[:, None] // step_size % 2 * (
            index_vals[None, :] // step_size % 2
        )
    return jnp.where(parity % 2 == 0, 1.0, -1.0).astype(jnp.float32) / math.sqrt(block_len)


def quantize(blocks, exps, table, signs):
    signed = blocks * (2.0 * signs.astype(jnp.float32) - 1.0)
    rotated = jnp.einsum("bnk,kj->bnj", signed, table, precision=lax.Precision.HIGHEST)
    factor = jnp.exp2(exps.astype(jnp.float32))[..., None]
    coded = jnp.clip(rotated / factor, -4.0, 4.0).astype(jnp.bfloat16)
    return (coded.astype(jnp.float32) * factor).astype(jnp.bfloat16)


def rotary_angles(values, positions):
    half_width = values.shape[-1] // 2
    freqs = jnp.power(
        500000.0, -(jnp.arange(half_width, dtype=jnp.float32) * 2.0 / values.shape[-1])
    )
    angles = positions.astype(jnp.float32).reshape((-1,) + (1,) * (values.ndim - 1)) * freqs
    cosine = jnp.cos(angles)
    sine = jnp.sin(angles)
    first_half = values[..., :half_width]
    second_half = values[..., half_width:]
    return jnp.concatenate(
        [first_half * cosine - second_half * sine, second_half * cosine + first_half * sine],
        axis=-1,
    )


def body(
    hidden_in,
    exponents,
    signs,
    lengths,
    w_query,
    key_value_weight,
    w_out,
    keys_cache,
    cached_value_rows,
):
    batch_all, local_feat = hidden_in.shape
    block_len = signs.shape[0]
    table = hadamard_table(block_len)
    widened = hidden_in.astype(jnp.float32)
    energy = lax.psum(jnp.sum(widened * widened, axis=1, keepdims=True), ("gx", "gy"))
    row_scale = lax.rsqrt(energy / MODEL_WIDTH + 1e-05)
    own_blocks = local_feat // block_len
    own_exps = lax.dynamic_slice_in_dim(exponents, lax.axis_index("gy") * own_blocks, own_blocks, 1)
    coded_own = quantize(
        (widened * row_scale).reshape(batch_all, own_blocks, block_len), own_exps, table, signs
    )
    gathered = lax.all_gather(coded_own.reshape(batch_all, local_feat), "gy", axis=1, tiled=True)
    query_cols = w_query.shape[1]
    kv_heads = key_value_weight.shape[1]
    head_dim = key_value_weight.shape[3]
    kv_flat = key_value_weight.reshape(key_value_weight.shape[0], kv_heads * 2 * head_dim)
    owners = batch_all // lax.axis_size("gx")
    partial_cols = lax.psum_scatter(
        jnp.concatenate(
            [
                jnp.dot(gathered, w_query, preferred_element_type=jnp.float32),
                jnp.dot(gathered, kv_flat, preferred_element_type=jnp.float32),
            ],
            axis=1,
        ),
        "gx",
        scatter_dimension=1,
        tiled=True,
    )
    mine = lax.all_to_all(partial_cols, "gx", split_axis=0, concat_axis=1, tiled=True)
    query_unrotated = mine[:, :query_cols].reshape(owners, kv_heads, -1, head_dim)
    key_value_unrotated = mine[:, query_cols:].reshape(owners, kv_heads, 2, head_dim)
    query_rotated = rotary_angles(query_unrotated, lengths).astype(jnp.bfloat16)
    key_new = rotary_angles(key_value_unrotated[:, :, 0], lengths).astype(jnp.bfloat16)
    value_new = key_value_unrotated[:, :, 1].astype(jnp.bfloat16)
    scale = 1.0 / math.sqrt(head_dim)
    scores = (
        jnp.einsum("bgrd,bgpd->bgrp", query_rotated, keys_cache, preferred_element_type=jnp.float32)
        * scale
    )
    fresh = (
        jnp.einsum("bgrd,bgd->bgr", query_rotated, key_new, preferred_element_type=jnp.float32)
        * scale
    )
    valid = (jnp.arange(keys_cache.shape[2], dtype=jnp.int32)[None, :] < lengths[:, None])[
        :, None, None, :
    ]
    masked = jnp.where(valid, scores, -1e30)
    top = jnp.maximum(jnp.max(masked, axis=-1), fresh)
    weights = jnp.where(valid, jnp.exp(masked - top[..., None]), 0.0)
    fresh_w = jnp.exp(fresh - top)
    total = jnp.sum(weights, axis=-1) + fresh_w
    probs = (weights / total[..., None]).astype(jnp.bfloat16)
    fresh_p = (fresh_w / total).astype(jnp.bfloat16)
    mixed = jnp.einsum(
        "bgrp,bgpd->bgrd", probs, cached_value_rows, preferred_element_type=jnp.float32
    )
    mixed = (
        mixed
        + fresh_p.astype(jnp.float32)[..., None] * value_new.astype(jnp.float32)[:, :, None, :]
    )
    attended = mixed.astype(jnp.bfloat16).reshape(owners, -1)
    terms = jnp.dot(
        lax.all_gather(attended, "gx", axis=0, tiled=True),
        w_out,
        preferred_element_type=jnp.float32,
    )
    summed = lax.psum_scatter(terms, "gy", scatter_dimension=1, tiled=True)
    return summed.astype(jnp.bfloat16)


def solution(mesh):
    in_specs = (
        P("group", ("gx", "gy")),
        P("group", "gx"),
        P(),
        P(("group", "gx")),
        P("gx", "gy"),
        P("gx", "gy", None, None),
        P("gy", "gx"),
        P(("group", "gx"), "gy", None, None),
        P(("group", "gx"), "gy", None, None),
    )
    out_specs = P("group", ("gx", "gy"))
    nx, ny = mesh.shape["gx"], mesh.shape["gy"]
    run = functools.partial(direct_body, nx, ny) if nx * ny <= 16 else body
    return jax.shard_map(run, mesh=mesh, in_specs=in_specs, out_specs=out_specs, check_vma=False)
```
